512 devices in a mesh: tm: 16 (over z), query: 8 (over y, core), rec: 4 (over x).
Axes of the slice: x: 4, y: 4, z: 16, core: 2. Of those that a mesh axis runs over, the one named last changes fastest.
Arguments:
- frames: bfloat16 [4, 8192, 1024], P('rec', 'tm'), may hold values from -100 to 100
- queries: bfloat16 [4096, 1024], P('query'), may hold values from -10 to 10
- kernel: float32 [33, 4096], P(None, 'query'), may hold values from 0.01 to 0.12
- labels: int32 [4, 8192], P('rec', 'tm'), may hold values from 0 to 4095
- lengths: int32 [4], P('rec'), may hold values from 2048 to 8192, as said below
Outputs:
- grad_frames: bfloat16 [4, 8192, 1024], P('rec', 'tm', 'query')
- grad_queries: bfloat16 [4096, 1024], P('query', 'rec')
- grad_kernel: float32 [33, 4096], P(None, 'query')
The draws below stay inside these ranges and needn't reach their ends.
Inputs may be any that keep to these rules, and one draw needn't show every extreme that they name: `lengths`: each entry counts the valid frames at the start of its recording; at least one recording has all 8192 frames valid.
All inputs are finite; a program needn't handle non-finite values.
Results may differ from the reference program's by a relative error of at most 0.0049.
Values sent between devices are 32-bit elements; how exact they have to be, the bound alone decides.
No kernel may reach another device: no remote copies, remote signals or barrier semaphores. Data moves between devices by JAX's collectives and lax.ppermute only.
A program may use at most 64 MiB of HBM per device.

```python
import math
import jax
import jax.numpy as jnp
from jax import lax

W = 1024
NQ = 4096
TAPS = 33
HALF = 16
FRAMES = 8192
RECS = 4
N_QUERY = 8


def base_tables(key):
    table = jnp.clip(jax.random.normal(jax.random.fold_in(key, 11), (NQ, W), jnp.float32), -4.0, 4.0)
    blocks = jax.random.permutation(jax.random.fold_in(key, 12), N_QUERY)
    row_block = jnp.arange(NQ) // (NQ // N_QUERY)
    col_block = jnp.arange(W) // (W // N_QUERY)
    boost = jnp.where(col_block[None, :] == blocks[row_block][:, None], 2.5, 1.0)
    table = (table * boost).astype(jnp.bfloat16).astype(jnp.float32)
    kernel = jnp.exp(jax.random.uniform(jax.random.fold_in(key, 13), (TAPS, NQ), jnp.float32, math.log(0.01), math.log(0.12)))
    return (table, kernel)


def draw_queries(key, part):
    table, kernel = base_tables(key)
    return table.astype(jnp.bfloat16)


def draw_kernel(key, part):
    table, kernel = base_tables(key)
    return kernel


def draw_frames(key, part):
    noise = jnp.clip(jax.random.normal(jax.random.fold_in(key, 21), (RECS, FRAMES, W), jnp.float32), -6.0, 6.0)
    return noise.astype(jnp.bfloat16)


def draw_lengths(key, part):
    counts = jax.random.randint(jax.random.fold_in(key, 41), (RECS,), FRAMES // 4, FRAMES + 1)
    full_one = jax.random.randint(jax.random.fold_in(key, 42), (), 0, RECS)
    return jnp.where(jnp.arange(RECS) == full_one, FRAMES, counts).astype(jnp.int32)


def plant(entries, rng, smallest, largest):
    index_at = [jax.random.randint(jax.random.fold_in(rng, axis), (), 0, length) for axis, length in enumerate(entries.shape)]
    longest = entries.shape.index(max(entries.shape))
    next_to = index_at[:longest] + [(index_at[longest] + 1) % entries.shape[longest]] + index_at[longest + 1:]
    return entries.at[tuple(index_at)].set(smallest).at[tuple(next_to)].set(largest)


def setup_inputs(seed: int = 0) -> dict:
    key_list = jax.random.split(jax.random.key(seed), 6)
    frames = draw_frames(jax.random.fold_in(key_list[5], 71), 0)
    queries = draw_queries(jax.random.fold_in(key_list[5], 71), 0)
    kernel = draw_kernel(jax.random.fold_in(key_list[5], 71), 0)
    labels = plant(jax.random.randint(key_list[3], (RECS, FRAMES), 0, NQ), jax.random.fold_in(key_list[3], 1), 0, NQ - 1).astype(jnp.int32)
    lengths = draw_lengths(jax.random.fold_in(key_list[5], 71), 0)
    return {"frames": frames, "queries": queries, "kernel": kernel, "labels": labels, "lengths": lengths}


def reference(frames, queries, kernel, labels, lengths):
    logit_scale = 10.0 / math.sqrt(W)
    query_ids = jnp.arange(NQ, dtype=jnp.int32)
    frame_ids = jnp.arange(FRAMES, dtype=jnp.int32)

    def one_record(record_items):
        frame_rows, label_ids, length_now = record_items
        is_valid = frame_ids < length_now
        scores = jnp.dot(frame_rows, queries.T, preferred_element_type=jnp.float32) * logit_scale
        scores = jnp.where(is_valid[:, None], scores, 0.0)
        padded = jnp.pad(scores, ((HALF, HALF), (0, 0)))
        smooth = jnp.zeros((FRAMES, NQ), jnp.float32)
        for offset in range(TAPS):
            smooth = smooth + kernel[offset][None, :] * padded[offset:offset + FRAMES]
        softmax_out = jax.nn.softmax(smooth, axis=1)
        positive = (label_ids[:, None] == query_ids[None, :]).astype(jnp.float32)
        map_grad = jnp.where(is_valid[:, None], softmax_out - positive, 0.0)
        grad_pad = jnp.pad(map_grad, ((HALF, HALF), (0, 0)))
        score_grad = jnp.zeros((FRAMES, NQ), jnp.float32)
        for offset in range(TAPS):
            begin_row = 2 * HALF - offset
            score_grad = score_grad + kernel[offset][None, :] * grad_pad[begin_row:begin_row + FRAMES]
        score_grad = jnp.where(is_valid[:, None], score_grad, 0.0).astype(jnp.bfloat16)
        frame_grad = (jnp.dot(score_grad, queries, preferred_element_type=jnp.float32) * logit_scale).astype(jnp.bfloat16)
        query_part = lax.dot_general(score_grad, frame_rows, (((0,), (0,)), ((), ())), preferred_element_type=jnp.float32)
        kernel_part = jnp.stack([lax.optimization_barrier(jnp.sum(map_grad * padded[offset:offset + FRAMES], axis=0)) for offset in range(TAPS)])
        return (frame_grad, query_part, kernel_part)
    grad_frames, query_parts, kernel_parts = lax.map(one_record, (frames, labels, lengths))
    grad_queries = (lax.optimization_barrier(jnp.sum(query_parts, axis=0)) * logit_scale).astype(jnp.bfloat16)
    return (grad_frames, grad_queries, lax.optimization_barrier(jnp.sum(kernel_parts, axis=0)))
```

```python
import math

import jax
import jax.numpy as jnp
from jax import lax
from jax.sharding import PartitionSpec as P


def with_halo(x, axis, width):
    peers, length = lax.axis_size(axis), x.shape[0]
    up = [(i, i + 1) for i in range(peers - 1)]
    down = [(j, i) for i, j in up]
    before = lax.ppermute(x[length - width :], axis, up)
    after = lax.ppermute(x[:width], axis, down)
    return jnp.concatenate([before, x, after], axis=0)


def tap_sum(kernel, padded, row_count, flipped):
    tap_count = kernel.shape[0]
    running = jnp.zeros((row_count, padded.shape[1]), jnp.float32)
    for offset in range(tap_count):
        begin_row = tap_count - 1 - offset if flipped else offset
        running = running + kernel[offset][None, :] * padded[begin_row : begin_row + row_count]
    return running


def row_softmax(smooth):
    local_top = jnp.max(smooth, axis=1)
    local_total = jnp.sum(jnp.exp(smooth - local_top[:, None]), axis=1)
    pairs = lax.all_gather(jnp.stack([local_top, local_total]), "query")
    tops, totals = pairs[:, 0], pairs[:, 1]
    top = jnp.max(tops, axis=0)
    total = jnp.sum(totals * jnp.exp(tops - top[None, :]), axis=0)
    return jnp.exp(smooth - top[:, None]) / total[:, None]


LANES = 128
TAP_ROWS = 16


def reduce_query_side(query_part, kernel_part):
    recs, tms = lax.axis_size("rec"), lax.axis_size("tm")
    queries, width = query_part.shape
    taps = kernel_part.shape[0]
    groups = queries // LANES
    halves = width // recs // LANES
    rows = queries // tms
    q = query_part.reshape(tms, rows, recs, halves, LANES)
    q = q.transpose(2, 0, 3, 1, 4).reshape(recs, tms, halves * rows, LANES)
    k = jnp.pad(kernel_part, ((0, tms * TAP_ROWS // groups - taps), (0, 0)))
    k = k.reshape(-1, groups, LANES).transpose(1, 0, 2).reshape(1, tms, TAP_ROWS, LANES)
    k = jnp.broadcast_to(k, (recs, tms, TAP_ROWS, LANES))
    chunks = jnp.concatenate([q, k], axis=2)
    chunks = jnp.sum(lax.all_to_all(chunks, "rec", 0, 0), axis=0)
    chunk = jnp.sum(lax.all_to_all(chunks, "tm", 0, 0), axis=0)
    whole = lax.all_gather(chunk, "tm")
    q = whole[:, : halves * rows].reshape(tms, halves, rows, LANES)
    q = q.transpose(0, 2, 1, 3).reshape(queries, width // recs)
    k = whole[:, halves * rows :].reshape(groups, tms * TAP_ROWS // groups, LANES)
    k = k.transpose(1, 0, 2).reshape(-1, queries)[:taps]
    return q, k


def per_device(frames, queries, kernel, labels, lengths):
    frame_rows = frames[0]
    label_ids = labels[0]
    length_now = lengths[0]
    row_count = frame_rows.shape[0]
    query_count = queries.shape[0]
    width = frame_rows.shape[1]
    tap_count = kernel.shape[0]
    rim_width = tap_count // 2
    logit_scale = 10.0 / math.sqrt(width)
    frame_start = lax.axis_index("tm") * row_count
    is_valid = frame_start + jnp.arange(row_count, dtype=jnp.int32) < length_now
    query_start = lax.axis_index("query") * query_count
    query_ids = query_start + jnp.arange(query_count, dtype=jnp.int32)
    scores = (
        lax.dot_general(
            frame_rows, queries, (((1,), (1,)), ((), ())), preferred_element_type=jnp.float32
        )
        * logit_scale
    )
    scores = jnp.where(is_valid[:, None], scores, 0.0)
    padded = with_halo(scores, "tm", rim_width)
    smooth = tap_sum(kernel, padded, row_count, False)
    softmax_out = row_softmax(smooth)
    positive = (label_ids[:, None] == query_ids[None, :]).astype(jnp.float32)
    map_grad = jnp.where(is_valid[:, None], softmax_out - positive, 0.0)
    grad_pad = with_halo(map_grad, "tm", rim_width)
    score_grad = tap_sum(kernel, grad_pad, row_count, True)
    score_grad = jnp.where(is_valid[:, None], score_grad, 0.0).astype(jnp.bfloat16)
    frame_part = jnp.dot(score_grad, queries, preferred_element_type=jnp.float32)
    query_part = lax.dot_general(
        score_grad, frame_rows, (((0,), (0,)), ((), ())), preferred_element_type=jnp.float32
    )
    kernel_part = jnp.stack(
        [
            jnp.sum(map_grad * padded[offset : offset + row_count], axis=0)
            for offset in range(tap_count)
        ]
    )
    frame_part, query_part, kernel_part = lax.optimization_barrier((frame_part, query_part, kernel_part))
    frame_sum = lax.psum_scatter(frame_part, "query", scatter_dimension=1, tiled=True)
    query_cols, grad_kernel = reduce_query_side(query_part, kernel_part)
    grad_frames = (frame_sum * logit_scale).astype(jnp.bfloat16)[None]
    grad_queries = (query_cols * logit_scale).astype(jnp.bfloat16)
    return (grad_frames, grad_queries, grad_kernel)


def solution(mesh):
    in_specs = (P("rec", "tm", None), P("query", None), P(None, "query"), P("rec", "tm"), P("rec"))
    out_specs = (P("rec", "tm", "query"), P("query", "rec"), P(None, "query"))
    return jax.shard_map(
        per_device, mesh=mesh, in_specs=in_specs, out_specs=out_specs, check_vma=False
    )
```

```python
import math

import jax
import jax.numpy as jnp
from jax import lax
from jax.experimental import pallas as pl
from jax.experimental.pallas import tpu as pltpu
from jax.sharding import PartitionSpec as P

SUB = 8
LANES = 128
VMEM = pltpu.VMEM
F32 = jnp.float32
UNIT = 8


def whole_spec(count):
    return [pl.BlockSpec(memory_space=VMEM)] * count


def params():
    return pltpu.CompilerParams(vmem_limit_bytes=48 * 1024 * 1024)


def cost(flops, bytes_accessed):
    return pl.CostEstimate(flops=flops, bytes_accessed=bytes_accessed, transcendentals=0)


def placement(rows, blk, flipped=False):
    m = lax.broadcasted_iota(jnp.int32, (rows, rows), 1 if flipped else 0)
    f = lax.broadcasted_iota(jnp.int32, (rows, rows), 0 if flipped else 1)
    return jnp.where(f == (m & (SUB - 1)) * blk + m // SUB, 1.0, 0.0).astype(jnp.bfloat16)


def dot_t(a, b):
    return lax.dot_general(a, b, (((1,), (1,)), ((), ())), preferred_element_type=F32)


def score_kernel(scale, scalars, frames, queries, out):
    rows = frames.shape[0]
    blk = rows // SUB
    placed = jnp.dot(placement(rows, blk), frames[...], preferred_element_type=F32).astype(jnp.bfloat16)
    m = lax.broadcasted_iota(jnp.int32, (rows, 1), 0)
    frame = scalars[0] + (m & (SUB - 1)) * blk + m // SUB
    out[...] = jnp.where(frame < scalars[1], dot_t(placed, queries[...]) * scale, 0.0)


def broadcast_taps(taps, wide, count):
    for j in range(count):
        wide[j] = jnp.broadcast_to(taps[j : j + 1, :], wide.shape[1:])


def tap_block(load, wide, g, count, flipped):
    sums = [None] * UNIT
    rows = [load(t) for t in range(UNIT + count - 1)]
    for j in range(count):
        tap = wide[count - 1 - j if flipped else j, :, g * LANES : (g + 1) * LANES]
        for u in range(UNIT):
            term = tap * rows[u + j]
            sums[u] = term if sums[u] is None else sums[u] + term
    return sums


def smooth_kernel(scale, half, scalars, main, before, after, queries, taps, scores, powers, stats, wide):
    blk = main.shape[0]
    count = 2 * half + 1
    groups = queries.shape[0] // LANES
    rim = 2 * half
    broadcast_taps(taps, wide, count)
    rim_frames = jnp.concatenate([before[:rim, :], after[:rim, :]], axis=0).astype(jnp.bfloat16)
    k = lax.broadcasted_iota(jnp.int32, (2 * rim, 1), 0)
    frame = scalars[0] + jnp.where(k < rim, k - rim, blk * SUB + k - rim)
    rim_scores = jnp.where(
        (frame >= 0) & (frame < scalars[1]), dot_t(rim_frames, queries[...]) * scale, 0.0
    )
    sub = lax.broadcasted_iota(jnp.int32, main.shape[1:], 0)
    scores[rim : rim + blk] = main[...]
    for t in range(rim):
        low = pltpu.roll(main[blk - rim + t], 1, 0)
        scores[t] = jnp.where(sub == 0, rim_scores[t : t + 1, :], low)
        high = pltpu.roll(main[t], SUB - 1, 0)
        scores[rim + blk + t] = jnp.where(sub == SUB - 1, rim_scores[rim + t : rim + t + 1, :], high)
    lane = lax.broadcasted_iota(jnp.int32, (SUB, LANES), 1)

    def step(b, carry):
        tops, totals = carry
        first = b * UNIT
        tiles = []
        for g in range(groups):
            cols = slice(g * LANES, (g + 1) * LANES)
            tiles.append(tap_block(lambda t: scores[first + t, :, cols], wide, g, count, False))
        for u in range(UNIT):
            mine = [tiles[g][u] for g in range(groups)]
            peak = mine[0]
            for tile in mine[1:]:
                peak = jnp.maximum(peak, tile)
            top = jnp.max(peak, axis=1, keepdims=True)
            total = None
            for g in range(groups):
                e = jnp.exp(mine[g] - top)
                powers[first + u, :, g * LANES : (g + 1) * LANES] = e
                total = e if total is None else total + e
            total = jnp.sum(total, axis=1, keepdims=True)
            here = lane == first + u
            tops = jnp.where(here, top, tops)
            totals = jnp.where(here, total, totals)
        return tops, totals

    zero = jnp.zeros((SUB, LANES), F32)
    tops, totals = lax.fori_loop(0, (blk + rim) // UNIT, step, (zero, zero))
    stats[0] = tops
    stats[1] = totals


def grad_kernel(
    half, chunk_rows, scalars, powers, scores, mine, others, labels, frames, queries, taps,
    chunks, frame_part, wide, grads, tap_grads, placed,
):
    blk = powers.shape[0] - 2 * half
    rows = blk * SUB
    count = 2 * half + 1
    width = queries.shape[1]
    query_count = queries.shape[0]
    groups = query_count // LANES
    broadcast_taps(taps, wide, count)
    tops = others[:, 0]
    top = jnp.max(tops, axis=0)
    total = jnp.sum(others[:, 1] * jnp.exp(tops - top[None]), axis=0)
    lane = lax.broadcasted_iota(jnp.int32, (SUB, LANES), 1)
    frame = scalars[0] + lax.broadcasted_iota(jnp.int32, (SUB, LANES), 0) * blk + lane - half
    valid = (frame >= 0) & (frame < scalars[1]) & (lane < blk + 2 * half)
    weight = jnp.where(valid, jnp.exp(mine[0] - top) / total, 0.0)
    label = jnp.where(valid, labels[...] - scalars[2].astype(F32), -1.0)
    keep = jnp.where(valid, 1.0, 0.0)
    ids = lax.broadcasted_iota(jnp.int32, (SUB, query_count), 1).astype(F32)

    def place(b, _):
        first = b * UNIT
        turn = lax.rem(LANES - first, LANES)
        w = pltpu.roll(weight, turn, 1)
        l = pltpu.roll(label, turn, 1)
        for u in range(UNIT):
            positive = jnp.where(ids == l[:, u : u + 1], 1.0, 0.0)
            grads[first + u] = powers[first + u] * w[:, u : u + 1] - positive * 1.0
        return 0

    lax.fori_loop(0, (blk + 2 * half) // UNIT, place, 0)
    tap_grads[...] = jnp.zeros_like(tap_grads)

    def correlate(b, _):
        first = half + b * UNIT
        for g in range(groups):
            cols = slice(g * LANES, (g + 1) * LANES)
            left = [grads[first + u, :, cols] for u in range(UNIT)]
            right = [scores[first + t, :, cols] for t in range(UNIT + count - 1)]
            for j in range(count):
                terms = [left[u] * right[u + j] for u in range(UNIT)]
                while len(terms) > 1:
                    terms = [terms[n] + terms[n + 1] for n in range(0, len(terms), 2)]
                tap_grads[j, :, cols] += terms[0]
        return 0

    lax.fori_loop(0, blk // UNIT, correlate, 0)

    def spread(b, _):
        first = b * UNIT
        turn = lax.rem(2 * LANES - half - first, LANES)
        kept = pltpu.roll(keep, turn, 1)
        for g in range(groups):
            cols = slice(g * LANES, (g + 1) * LANES)
            sums = tap_block(lambda t: grads[first + t, :, cols], wide, g, count, True)
            sums = [sums[u] * kept[:, u : u + 1] for u in range(UNIT)]
            block = jnp.concatenate(sums, axis=0).astype(jnp.bfloat16)
            placed[pl.ds(pl.multiple_of(first * SUB, UNIT * SUB), UNIT * SUB), cols] = block
        return 0

    lax.fori_loop(0, blk // UNIT, spread, 0)
    score_grad = jnp.dot(placement(rows, blk, True), placed[...], preferred_element_type=F32)
    frame_part[...] = jnp.dot(score_grad.astype(jnp.bfloat16), queries[...], preferred_element_type=F32)
    turned = score_grad.T.astype(jnp.bfloat16)
    recs, tms, padded_rows, part_width = chunks.shape
    parts = jnp.sum(tap_grads[...], axis=1)
    parts = jnp.concatenate([parts, jnp.zeros((padded_rows_of(count) - count, query_count), F32)], axis=0)
    tap_rows = padded_rows - chunk_rows
    halves = query_count // part_width
    per_half = tms // halves
    for r in range(recs):
        part = jnp.dot(turned, frames[:, r * part_width : (r + 1) * part_width], preferred_element_type=F32)
        for z in range(tms):
            chunks[r, z, :chunk_rows, :] = part[z * chunk_rows : (z + 1) * chunk_rows, :]
            start = (z % per_half) * tap_rows
            h = z // per_half
            if start < count:
                chunks[r, z, chunk_rows:, :] = parts[
                    start : start + tap_rows, h * part_width : (h + 1) * part_width
                ]
            else:
                chunks[r, z, chunk_rows:, :] = jnp.zeros((tap_rows, part_width), F32)


def padded_rows_of(count):
    return (count + UNIT - 1) // UNIT * UNIT


def per_device(frames, queries, kernel, labels, lengths):
    frame_rows = frames[0]
    label_ids = labels[0].astype(F32)
    rows, width = frame_rows.shape
    query_count = queries.shape[0]
    count = kernel.shape[0]
    half = count // 2
    rim = 2 * half
    blk = rows // SUB
    scale = 10.0 / math.sqrt(width)
    recs, tms, blocks = lax.axis_size("rec"), lax.axis_size("tm"), lax.axis_size("query")
    scalars = jnp.stack(
        [lax.axis_index("tm") * rows, lengths[0], lax.axis_index("query") * query_count]
    ).astype(jnp.int32)
    smem = pl.BlockSpec(memory_space=pltpu.SMEM)

    def edge(part, ids):
        extra = jnp.pad(ids[None, :], ((0, UNIT - 1), (0, width - rim)))
        return jnp.concatenate([part.astype(F32), extra], axis=0)

    up = [(i, i + 1) for i in range(tms - 1)]
    down = [(j, i) for i, j in up]
    before = lax.ppermute(edge(frame_rows[rows - rim :], label_ids[rows - rim :]), "tm", up)
    after = lax.ppermute(edge(frame_rows[:rim], label_ids[:rim]), "tm", down)
    main = pl.pallas_call(
        lambda *refs: score_kernel(scale, *refs),
        out_shape=jax.ShapeDtypeStruct((rows, query_count), F32),
        in_specs=[smem] + whole_spec(2),
        out_specs=pl.BlockSpec(memory_space=VMEM),
        compiler_params=params(),
        cost_estimate=cost(2 * rows * width * (rows + query_count), 3 << 20),
    )(scalars, frame_rows, queries)
    main = main.reshape(blk, SUB, query_count)
    scores, powers, stats = pl.pallas_call(
        lambda *refs: smooth_kernel(scale, half, *refs),
        out_shape=[
            jax.ShapeDtypeStruct((blk + 2 * rim, SUB, query_count), F32),
            jax.ShapeDtypeStruct((blk + rim, SUB, query_count), F32),
            jax.ShapeDtypeStruct((2, SUB, LANES), F32),
        ],
        in_specs=[smem] + whole_spec(5),
        out_specs=whole_spec(3),
        scratch_shapes=[VMEM((count, SUB, query_count), F32)],
        compiler_params=params(),
        cost_estimate=cost(4 * rows * query_count * count, 6 << 20),
    )(scalars, main, before, after, queries, kernel)
    others = lax.all_to_all(jnp.broadcast_to(stats[None], (blocks,) + stats.shape), "query", 0, 0)
    ext = jnp.concatenate([before[rim, half:rim], label_ids, after[rim, :half], jnp.zeros((blk - rim,), F32)])
    ext = ext.reshape(SUB + 1, blk)
    tile = jnp.concatenate([ext[:SUB], ext[1:, :rim], jnp.zeros((SUB, LANES - blk - rim), F32)], axis=1)
    chunk_rows = query_count // tms
    part_width = width // recs
    chunks, frame_part = pl.pallas_call(
        lambda *refs: grad_kernel(half, chunk_rows, *refs),
        out_shape=[
            jax.ShapeDtypeStruct((recs, tms, chunk_rows + UNIT, part_width), F32),
            jax.ShapeDtypeStruct((rows, width), F32),
        ],
        in_specs=[smem] + whole_spec(8),
        out_specs=whole_spec(2),
        scratch_shapes=[
            VMEM((count, SUB, query_count), F32),
            VMEM((blk + rim, SUB, query_count), F32),
            VMEM((count, SUB, query_count), F32),
            VMEM((rows, query_count), jnp.bfloat16),
        ],
        compiler_params=params(),
        cost_estimate=cost(4 * rows * query_count * (width + 2 * count), 12 << 20),
    )(scalars, powers, scores, stats, others, tile, frame_rows, queries, kernel)
    frame_sum = lax.psum_scatter(frame_part, "query", scatter_dimension=1, tiled=True)
    chunks = jnp.sum(lax.all_to_all(chunks, "rec", 0, 0), axis=0)
    chunk = jnp.sum(lax.all_to_all(chunks, "tm", 0, 0), axis=0)
    whole = lax.all_gather(chunk, "tm")
    query_sum = whole[:, :chunk_rows].reshape(query_count, part_width)
    halves = query_count // part_width
    tap_sum = whole[:, chunk_rows:].reshape(halves, tms // halves * UNIT, part_width)
    tap_sum = jnp.concatenate([tap_sum[h, :count] for h in range(halves)], axis=1)
    grad_frames = (frame_sum * scale).astype(jnp.bfloat16)[None]
    grad_queries = (query_sum * scale).astype(jnp.bfloat16)
    return (grad_frames, grad_queries, tap_sum)


def solution(mesh):
    in_specs = (P("rec", "tm", None), P("query", None), P(None, "query"), P("rec", "tm"), P("rec"))
    out_specs = (P("rec", "tm", "query"), P("query", "rec"), P(None, "query"))
    return jax.shard_map(
        per_device, mesh=mesh, in_specs=in_specs, out_specs=out_specs, check_vma=False
    )
```

```python
import math

import jax
import jax.numpy as jnp
from jax import lax
from jax.experimental import pallas as pl
from jax.experimental.pallas import tpu as pltpu
from jax.sharding import PartitionSpec as P

SUB = 8
LANES = 128
VMEM = pltpu.VMEM
F32 = jnp.float32
UNIT = 8


def whole_spec(count):
    return [pl.BlockSpec(memory_space=VMEM)] * count


def params(mib):
    return pltpu.CompilerParams(vmem_limit_bytes=mib << 20)


def cost(flops, bytes_accessed):
    return pl.CostEstimate(flops=flops, bytes_accessed=bytes_accessed, transcendentals=0)


def placement(rows, blk, flipped=False):
    m = lax.broadcasted_iota(jnp.int32, (rows, rows), 1 if flipped else 0)
    f = lax.broadcasted_iota(jnp.int32, (rows, rows), 0 if flipped else 1)
    return jnp.where(f == (m & (SUB - 1)) * blk + m // SUB, 1.0, 0.0).astype(jnp.bfloat16)


def dot_t(a, b):
    return lax.dot_general(a, b, (((1,), (1,)), ((), ())), preferred_element_type=F32)


def score_kernel(scale, scalars, frames, queries, out):
    rows = frames.shape[0]
    blk = rows // SUB
    placed = jnp.dot(placement(rows, blk), frames[...], preferred_element_type=F32).astype(jnp.bfloat16)
    m = lax.broadcasted_iota(jnp.int32, (rows, 1), 0)
    frame = scalars[0] + (m & (SUB - 1)) * blk + m // SUB
    out[...] = jnp.where(frame < scalars[1], dot_t(placed, queries[...]) * scale, 0.0)


def broadcast_taps(taps, wide, count):
    for j in range(count):
        wide[j] = jnp.broadcast_to(taps[j : j + 1, :], wide.shape[1:])


def tap_block(load, wide, g, count, flipped):
    sums = [None] * UNIT
    rows = [load(t) for t in range(UNIT + count - 1)]
    for j in range(count):
        tap = wide[count - 1 - j if flipped else j, :, g * LANES : (g + 1) * LANES]
        for u in range(UNIT):
            term = tap * rows[u + j]
            sums[u] = term if sums[u] is None else sums[u] + term
    return sums


def smooth_kernel(scale, half, scalars, main, before, after, queries, taps, scores, powers, stats, wide):
    blk = main.shape[0]
    count = 2 * half + 1
    groups = queries.shape[0] // LANES
    rim = 2 * half
    broadcast_taps(taps, wide, count)
    rim_frames = jnp.concatenate([before[:rim, :], after[:rim, :]], axis=0).astype(jnp.bfloat16)
    k = lax.broadcasted_iota(jnp.int32, (2 * rim, 1), 0)
    frame = scalars[0] + jnp.where(k < rim, k - rim, blk * SUB + k - rim)
    rim_scores = jnp.where(
        (frame >= 0) & (frame < scalars[1]), dot_t(rim_frames, queries[...]) * scale, 0.0
    )
    sub = lax.broadcasted_iota(jnp.int32, main.shape[1:], 0)
    scores[rim : rim + blk] = main[...]
    for t in range(rim):
        low = pltpu.roll(main[blk - rim + t], 1, 0)
        scores[t] = jnp.where(sub == 0, rim_scores[t : t + 1, :], low)
        high = pltpu.roll(main[t], SUB - 1, 0)
        scores[rim + blk + t] = jnp.where(sub == SUB - 1, rim_scores[rim + t : rim + t + 1, :], high)
    lane = lax.broadcasted_iota(jnp.int32, (SUB, LANES), 1)

    def step(b, carry):
        tops, totals = carry
        first = b * UNIT
        tiles = []
        for g in range(groups):
            cols = slice(g * LANES, (g + 1) * LANES)
            tiles.append(tap_block(lambda t: scores[first + t, :, cols], wide, g, count, False))
        for u in range(UNIT):
            mine = [tiles[g][u] for g in range(groups)]
            peak = mine[0]
            for tile in mine[1:]:
                peak = jnp.maximum(peak, tile)
            top = jnp.max(peak, axis=1, keepdims=True)
            total = None
            for g in range(groups):
                e = jnp.exp(mine[g] - top)
                powers[first + u, :, g * LANES : (g + 1) * LANES] = e
                total = e if total is None else total + e
            total = jnp.sum(total, axis=1, keepdims=True)
            here = lane == first + u
            tops = jnp.where(here, top, tops)
            totals = jnp.where(here, total, totals)
        return tops, totals

    zero = jnp.zeros((SUB, LANES), F32)
    tops, totals = lax.fori_loop(0, (blk + rim) // UNIT, step, (zero, zero))
    stats[0] = tops
    stats[1] = totals


def grad_kernel(
    half, scalars, powers, mine, others, labels, frames, taps, grads, score_grad, ahead, behind, wide, placed,
):
    blk = powers.shape[0] - 2 * half
    rows = blk * SUB
    count = 2 * half + 1
    query_count = taps.shape[1]
    groups = query_count // LANES
    broadcast_taps(taps, wide, count)
    tops = others[:, 0]
    top = jnp.max(tops, axis=0)
    total = jnp.sum(others[:, 1] * jnp.exp(tops - top[None]), axis=0)
    lane = lax.broadcasted_iota(jnp.int32, (SUB, LANES), 1)
    frame = scalars[0] + lax.broadcasted_iota(jnp.int32, (SUB, LANES), 0) * blk + lane - half
    valid = (frame >= 0) & (frame < scalars[1]) & (lane < blk + 2 * half)
    weight = jnp.where(valid, jnp.exp(mine[0] - top) / total, 0.0)
    label = jnp.where(valid, labels[...] - scalars[2].astype(F32), -1.0)
    keep = jnp.where(valid, 1.0, 0.0)
    ids = lax.broadcasted_iota(jnp.int32, (SUB, query_count), 1).astype(F32)

    def place(b, _):
        first = b * UNIT
        turn = lax.rem(LANES - first, LANES)
        w = pltpu.roll(weight, turn, 1)
        l = pltpu.roll(label, turn, 1)
        for u in range(UNIT):
            positive = jnp.where(ids == l[:, u : u + 1], 1.0, 0.0)
            grads[first + u] = powers[first + u] * w[:, u : u + 1] - positive
        return 0

    lax.fori_loop(0, (blk + 2 * half) // UNIT, place, 0)

    def spread(b, _):
        first = b * UNIT
        turn = lax.rem(2 * LANES - half - first, LANES)
        kept = pltpu.roll(keep, turn, 1)
        for g in range(groups):
            cols = slice(g * LANES, (g + 1) * LANES)
            sums = tap_block(lambda t: grads[first + t, :, cols], wide, g, count, True)
            sums = [sums[u] * kept[:, u : u + 1] for u in range(UNIT)]
            block = jnp.concatenate(sums, axis=0).astype(jnp.bfloat16)
            placed[pl.ds(pl.multiple_of(first * SUB, UNIT * SUB), UNIT * SUB), cols] = block
        return 0

    lax.fori_loop(0, blk // UNIT, spread, 0)
    natural = jnp.dot(placement(rows, blk, True), placed[...], preferred_element_type=F32)
    natural = natural.astype(jnp.bfloat16)
    score_grad[...] = natural
    far = column_block(frames, scalars[5], ahead.shape[1])
    part = jnp.dot(turn_over(natural), far, preferred_element_type=F32)
    ahead[...] = part[: query_count // 2]
    behind[...] = part[query_count // 2 :]


def column_block(frames, index, width):
    return frames[:, pl.ds(pl.multiple_of(index * width, LANES), width)]


def turn_over(score_grad):
    return score_grad.astype(F32).T.astype(jnp.bfloat16)


def own_kernel(half, scalars, grads, scores, score_grad, frames, own, taps_out, tap_grads):
    blk = grads.shape[0] - 2 * half
    count = 2 * half + 1
    query_count = score_grad.shape[1]
    groups = query_count // LANES
    tap_grads[...] = jnp.zeros_like(tap_grads)

    def correlate(b, _):
        first = half + b * UNIT
        for g in range(groups):
            cols = slice(g * LANES, (g + 1) * LANES)
            left = [grads[first + u, :, cols] for u in range(UNIT)]
            right = [scores[first + t, :, cols] for t in range(UNIT + count - 1)]
            for j in range(count):
                terms = [left[u] * right[u + j] for u in range(UNIT)]
                while len(terms) > 1:
                    terms = [terms[n] + terms[n + 1] for n in range(0, len(terms), 2)]
                tap_grads[j, :, cols] += terms[0]
        return 0

    lax.fori_loop(0, blk // UNIT, correlate, 0)
    parts = jnp.sum(tap_grads[...], axis=1)
    tall = padded_rows_of(count)
    parts = jnp.concatenate([parts, jnp.zeros((tall - count, query_count), F32)], axis=0)
    part_width = own.shape[1]
    for h in range(query_count // part_width):
        taps_out[h * tall : (h + 1) * tall, :] = parts[:, h * part_width : (h + 1) * part_width]
    mine = column_block(frames, scalars[3], part_width)
    own[...] = jnp.dot(turn_over(score_grad[...]), mine, preferred_element_type=F32)


def near_kernel(scalars, score_grad, frames, queries, taps_in, from_behind, from_ahead, ahead, behind, frame_part):
    query_count = score_grad.shape[1]
    part_width = ahead.shape[1]
    middle = query_count // 2
    turned = turn_over(score_grad[...])
    part = jnp.dot(turned, column_block(frames, scalars[4], part_width), preferred_element_type=F32)
    ahead[:middle, :] = part[:middle] + from_behind[...]
    ahead[middle:query_count, :] = part[middle:]
    ahead[query_count:, :] = taps_in[...]
    part = jnp.dot(turned, column_block(frames, scalars[6], part_width), preferred_element_type=F32)
    behind[:middle, :] = part[:middle]
    behind[middle:query_count, :] = part[middle:] + from_ahead[...]
    behind[query_count:, :] = taps_in[...]
    frame_part[...] = jnp.dot(score_grad[...], queries[...], preferred_element_type=F32)


def sum_kernel(own, taps_own, from_behind, from_ahead, taps_far, chunks):
    tms, padded_rows, _ = chunks.shape
    query_count = own.shape[0]
    chunk_rows = query_count // tms
    tap_rows = padded_rows - chunk_rows
    for z in range(tms):
        rows = slice(z * chunk_rows, (z + 1) * chunk_rows)
        chunks[z, :chunk_rows, :] = own[rows, :] + from_behind[rows, :] + from_ahead[rows, :]
        if z * tap_rows < taps_own.shape[0]:
            rows = slice(z * tap_rows, (z + 1) * tap_rows)
            late = slice(query_count + z * tap_rows, query_count + (z + 1) * tap_rows)
            chunks[z, chunk_rows:, :] = (
                taps_own[rows, :] + taps_far[rows, :] + from_behind[late, :] + from_ahead[late, :]
            )
        else:
            chunks[z, chunk_rows:, :] = jnp.zeros((tap_rows, own.shape[1]), F32)


def padded_rows_of(count):
    return (count + UNIT - 1) // UNIT * UNIT


def per_device(frames, queries, kernel, labels, lengths):
    frame_rows = frames[0]
    label_ids = labels[0].astype(F32)
    rows, width = frame_rows.shape
    query_count = queries.shape[0]
    count = kernel.shape[0]
    half = count // 2
    rim = 2 * half
    blk = rows // SUB
    scale = 10.0 / math.sqrt(width)
    recs, tms, blocks = lax.axis_size("rec"), lax.axis_size("tm"), lax.axis_size("query")
    rec = lax.axis_index("rec")
    ring = [(rec + step) % recs for step in range(4)]
    scalars = jnp.stack(
        [lax.axis_index("tm") * rows, lengths[0], lax.axis_index("query") * query_count] + ring
    ).astype(jnp.int32)
    smem = pl.BlockSpec(memory_space=pltpu.SMEM)

    def edge(part, ids):
        extra = jnp.pad(ids[None, :], ((0, UNIT - 1), (0, width - rim)))
        return jnp.concatenate([part.astype(F32), extra], axis=0)

    up = [(i, i + 1) for i in range(tms - 1)]
    down = [(j, i) for i, j in up]
    before = lax.ppermute(edge(frame_rows[rows - rim :], label_ids[rows - rim :]), "tm", up)
    after = lax.ppermute(edge(frame_rows[:rim], label_ids[:rim]), "tm", down)
    main = pl.pallas_call(
        lambda *refs: score_kernel(scale, *refs),
        out_shape=jax.ShapeDtypeStruct((rows, query_count), F32),
        in_specs=[smem] + whole_spec(2),
        out_specs=pl.BlockSpec(memory_space=VMEM),
        compiler_params=params(12),
        cost_estimate=cost(2 * rows * width * (rows + query_count), 3 << 20),
    )(scalars, frame_rows, queries)
    main = main.reshape(blk, SUB, query_count)
    scores, powers, stats = pl.pallas_call(
        lambda *refs: smooth_kernel(scale, half, *refs),
        out_shape=[
            jax.ShapeDtypeStruct((blk + 2 * rim, SUB, query_count), F32),
            jax.ShapeDtypeStruct((blk + rim, SUB, query_count), F32),
            jax.ShapeDtypeStruct((2, SUB, LANES), F32),
        ],
        in_specs=[smem] + whole_spec(5),
        out_specs=whole_spec(3),
        scratch_shapes=[VMEM((count, SUB, query_count), F32)],
        compiler_params=params(12),
        cost_estimate=cost(4 * rows * query_count * count, 6 << 20),
    )(scalars, main, before, after, queries, kernel)
    ext = jnp.concatenate([before[rim, half:rim], label_ids, after[rim, :half], jnp.zeros((blk - rim,), F32)])
    ext = ext.reshape(SUB + 1, blk)
    tile = jnp.concatenate([ext[:SUB], ext[1:, :rim], jnp.zeros((SUB, LANES - blk - rim), F32)], axis=1)
    stats, tile = lax.optimization_barrier((stats, tile))
    others = lax.all_to_all(jnp.broadcast_to(stats[None], (blocks,) + stats.shape), "query", 0, 0)
    chunk_rows = query_count // tms
    part_width = width // recs
    middle = query_count // 2
    grads, score_grad, far_a, far_b = pl.pallas_call(
        lambda *refs: grad_kernel(half, *refs),
        out_shape=[
            jax.ShapeDtypeStruct((blk + rim, SUB, query_count), F32),
            jax.ShapeDtypeStruct((rows, query_count), jnp.bfloat16),
            jax.ShapeDtypeStruct((middle, part_width), F32),
            jax.ShapeDtypeStruct((query_count - middle, part_width), F32),
        ],
        in_specs=[smem] + whole_spec(6),
        out_specs=whole_spec(4),
        scratch_shapes=[
            VMEM((count, SUB, query_count), F32),
            VMEM((rows, query_count), jnp.bfloat16),
        ],
        compiler_params=params(16),
        cost_estimate=cost(2 * rows * query_count * (width + 2 * count), 8 << 20),
    )(scalars, powers, stats, others, tile, frame_rows, kernel)
    onward = [(i, (i + 1) % recs) for i in range(recs)]
    back = [(j, i) for i, j in onward]
    far_a = lax.ppermute(far_a, "rec", onward)
    far_b = lax.ppermute(far_b, "rec", back)
    halves = query_count // part_width
    tap_rows = halves * padded_rows_of(count)
    own, taps_own = pl.pallas_call(
        lambda *refs: own_kernel(half, *refs),
        out_shape=[
            jax.ShapeDtypeStruct((query_count, part_width), F32),
            jax.ShapeDtypeStruct((tap_rows, part_width), F32),
        ],
        in_specs=[smem] + whole_spec(4),
        out_specs=whole_spec(2),
        scratch_shapes=[VMEM((count, SUB, query_count), F32)],
        compiler_params=params(16),
        cost_estimate=cost(4 * rows * query_count * (width + 2 * count), 16 << 20),
    )(scalars, grads, scores, score_grad, frame_rows)
    across = [(i, (i + 2) % recs) for i in range(recs)]
    taps_far = lax.ppermute(taps_own, "rec", across)
    near = jax.ShapeDtypeStruct((query_count + tap_rows, part_width), F32)
    near_a, near_b, frame_part = pl.pallas_call(
        near_kernel,
        out_shape=[near, near, jax.ShapeDtypeStruct((rows, width), F32)],
        in_specs=[smem] + whole_spec(6),
        out_specs=whole_spec(3),
        compiler_params=params(12),
        cost_estimate=cost(rows * query_count * width, 4 << 20),
    )(scalars, score_grad, frame_rows, queries, taps_own, far_a, far_b)
    frame_sum = lax.psum_scatter(frame_part, "query", scatter_dimension=1, tiled=True)
    near_a = lax.ppermute(near_a, "rec", onward)
    near_b = lax.ppermute(near_b, "rec", back)
    chunks = pl.pallas_call(
        sum_kernel,
        out_shape=jax.ShapeDtypeStruct((tms, chunk_rows + UNIT, part_width), F32),
        in_specs=whole_spec(5),
        out_specs=pl.BlockSpec(memory_space=VMEM),
        compiler_params=params(8),
        cost_estimate=cost(4 * query_count * part_width, 4 << 20),
    )(own, taps_own, near_a, near_b, taps_far)
    chunk = jnp.sum(lax.all_to_all(chunks, "tm", 0, 0), axis=0)
    frame_sum, chunk = lax.optimization_barrier((frame_sum, chunk))
    whole = lax.all_gather(chunk, "tm")
    query_sum = whole[:, :chunk_rows].reshape(query_count, part_width)
    tap_sum = whole[: tap_rows // UNIT, chunk_rows:].reshape(halves, tap_rows // halves, part_width)
    tap_sum = jnp.concatenate([tap_sum[h, :count] for h in range(halves)], axis=1)
    grad_frames = (frame_sum * scale).astype(jnp.bfloat16)[None]
    grad_queries = (query_sum * scale).astype(jnp.bfloat16)
    return (grad_frames, grad_queries, tap_sum)


def solution(mesh):
    in_specs = (P("rec", "tm", None), P("query", None), P(None, "query"), P("rec", "tm"), P("rec"))
    out_specs = (P("rec", "tm", "query"), P("query", "rec"), P(None, "query"))
    return jax.shard_map(
        per_device, mesh=mesh, in_specs=in_specs, out_specs=out_specs, check_vma=False
    )
```

```python
import math

import jax
import jax.numpy as jnp
from jax import lax
from jax.experimental import pallas as pl
from jax.experimental.pallas import tpu as pltpu
from jax.sharding import PartitionSpec as P

SUB = 8
LANES = 128
VMEM = pltpu.VMEM
F32 = jnp.float32
UNIT = 8


def whole_spec(count):
    return [pl.BlockSpec(memory_space=VMEM)] * count


def params(mib):
    return pltpu.CompilerParams(vmem_limit_bytes=mib << 20)


def cost(flops, bytes_accessed):
    return pl.CostEstimate(flops=flops, bytes_accessed=bytes_accessed, transcendentals=0)


def placement(rows, blk, flipped=False):
    m = lax.broadcasted_iota(jnp.int32, (rows, rows), 1 if flipped else 0)
    f = lax.broadcasted_iota(jnp.int32, (rows, rows), 0 if flipped else 1)
    return jnp.where(f == (m & (SUB - 1)) * blk + m // SUB, 1.0, 0.0).astype(jnp.bfloat16)


def dot_t(a, b):
    return lax.dot_general(a, b, (((1,), (1,)), ((), ())), preferred_element_type=F32)


def edge_kernel(half, last, first, labels, up, down):
    rim = 2 * half
    up[:rim, :] = last[...].astype(F32)
    down[:rim, :] = first[...].astype(F32)
    width = labels.shape[1]
    tail = labels[:, width - LANES :].astype(F32)
    up[rim:, :LANES] = jnp.broadcast_to(pltpu.roll(tail, half, 1), (UNIT, LANES))
    down[rim:, :LANES] = jnp.broadcast_to(labels[:, :LANES].astype(F32), (UNIT, LANES))


def score_kernel(scale, steps, scalars, frames, queries, out, place):
    rows = frames.shape[0]
    blk = rows // SUB
    step = pl.program_id(0)

    @pl.when(step == 0)
    def _():
        place[...] = placement(rows, blk)

    placed = jnp.dot(place[...], frames[...], preferred_element_type=F32).astype(jnp.bfloat16)
    term = dot_t(placed, queries[...])

    @pl.when(step == 0)
    def _():
        out[...] = term

    @pl.when(step > 0)
    def _():
        out[...] += term

    @pl.when(step == steps - 1)
    def _():
        m = lax.broadcasted_iota(jnp.int32, (rows, 1), 0)
        frame = scalars[0] + (m & (SUB - 1)) * blk + m // SUB
        out[...] = jnp.where(frame < scalars[1], out[...] * scale, 0.0)


def label_tile(half, blk, labels, before, after):
    rim = 2 * half
    sub = lax.broadcasted_iota(jnp.int32, (SUB, LANES), 0)
    lane = lax.broadcasted_iota(jnp.int32, (SUB, LANES), 1)
    base = jnp.zeros((SUB, LANES), F32)
    for s in range(SUB):
        at = s * blk
        row = labels[:, at // LANES * LANES : at // LANES * LANES + LANES].astype(F32)
        row = jnp.broadcast_to(row, (SUB, LANES))
        if at % LANES:
            row = pltpu.roll(row, LANES - at % LANES, 1)
        base = jnp.where(sub == s, row, base)
    low = pltpu.roll(pltpu.roll(base, LANES - blk + half, 1), 1, 0)
    low = jnp.where(sub == 0, before[rim:, :LANES], low)
    high = pltpu.roll(pltpu.roll(base, half + blk, 1), SUB - 1, 0)
    high = jnp.where(sub == SUB - 1, pltpu.roll(after[rim:, :LANES], half + blk, 1), high)
    tile = jnp.where(lane < half, low, pltpu.roll(base, half, 1))
    return jnp.where(lane >= half + blk, high, tile)


def broadcast_taps(taps, wide, count):
    for j in range(count):
        wide[j] = jnp.broadcast_to(taps[j : j + 1, :], wide.shape[1:])


def tap_block(load, wide, g, count, flipped):
    sums = [None] * UNIT
    rows = [load(t) for t in range(UNIT + count - 1)]
    for j in range(count):
        tap = wide[count - 1 - j if flipped else j, :, g * LANES : (g + 1) * LANES]
        for u in range(UNIT):
            term = tap * rows[u + j]
            sums[u] = term if sums[u] is None else sums[u] + term
    return sums


def smooth_kernel(
    scale, half, scalars, main, before, after, labels, queries, taps, scores, powers, stats, tile, wide
):
    blk = main.shape[0]
    count = 2 * half + 1
    groups = queries.shape[0] // LANES
    rim = 2 * half
    broadcast_taps(taps, wide, count)
    tile[...] = label_tile(half, blk, labels, before, after)
    rim_frames = jnp.concatenate([before[:rim, :], after[:rim, :]], axis=0).astype(jnp.bfloat16)
    k = lax.broadcasted_iota(jnp.int32, (2 * rim, 1), 0)
    frame = scalars[0] + jnp.where(k < rim, k - rim, blk * SUB + k - rim)
    rim_scores = jnp.where(
        (frame >= 0) & (frame < scalars[1]), dot_t(rim_frames, queries[...]) * scale, 0.0
    )
    sub = lax.broadcasted_iota(jnp.int32, main.shape[1:], 0)
    scores[rim : rim + blk] = main[...]
    for t in range(rim):
        low = pltpu.roll(main[blk - rim + t], 1, 0)
        scores[t] = jnp.where(sub == 0, rim_scores[t : t + 1, :], low)
        high = pltpu.roll(main[t], SUB - 1, 0)
        scores[rim + blk + t] = jnp.where(sub == SUB - 1, rim_scores[rim + t : rim + t + 1, :], high)
    lane = lax.broadcasted_iota(jnp.int32, (SUB, LANES), 1)

    def step(b, carry):
        tops, totals = carry
        first = b * UNIT
        tiles = []
        for g in range(groups):
            cols = slice(g * LANES, (g + 1) * LANES)
            tiles.append(tap_block(lambda t: scores[first + t, :, cols], wide, g, count, False))
        for u in range(UNIT):
            mine = [tiles[g][u] for g in range(groups)]
            peak = mine[0]
            for tile in mine[1:]:
                peak = jnp.maximum(peak, tile)
            top = jnp.max(peak, axis=1, keepdims=True)
            total = None
            for g in range(groups):
                e = jnp.exp(mine[g] - top)
                powers[first + u, :, g * LANES : (g + 1) * LANES] = e
                total = e if total is None else total + e
            total = jnp.sum(total, axis=1, keepdims=True)
            here = lane == first + u
            tops = jnp.where(here, top, tops)
            totals = jnp.where(here, total, totals)
        return tops, totals

    zero = jnp.zeros((SUB, LANES), F32)
    tops, totals = lax.fori_loop(0, (blk + rim) // UNIT, step, (zero, zero))
    stats[0] = tops
    stats[1] = totals


def grad_kernel(
    half, scalars, powers, mine, others, labels, frames, taps, grads, score_grad, ahead, behind, wide, placed,
):
    blk = powers.shape[0] - 2 * half
    rows = blk * SUB
    count = 2 * half + 1
    query_count = taps.shape[1]
    groups = query_count // LANES
    broadcast_taps(taps, wide, count)
    tops = others[:, 0]
    top = jnp.max(tops, axis=0)
    total = jnp.sum(others[:, 1] * jnp.exp(tops - top[None]), axis=0)
    lane = lax.broadcasted_iota(jnp.int32, (SUB, LANES), 1)
    frame = scalars[0] + lax.broadcasted_iota(jnp.int32, (SUB, LANES), 0) * blk + lane - half
    valid = (frame >= 0) & (frame < scalars[1]) & (lane < blk + 2 * half)
    weight = jnp.where(valid, jnp.exp(mine[0] - top) / total, 0.0)
    label = jnp.where(valid, labels[...] - scalars[2].astype(F32), -1.0)
    keep = jnp.where(valid, 1.0, 0.0)
    ids = lax.broadcasted_iota(jnp.int32, (SUB, query_count), 1).astype(F32)

    def place(b, _):
        first = b * UNIT
        turn = lax.rem(LANES - first, LANES)
        w = pltpu.roll(weight, turn, 1)
        l = pltpu.roll(label, turn, 1)
        for u in range(UNIT):
            positive = jnp.where(ids == l[:, u : u + 1], 1.0, 0.0)
            grads[first + u] = powers[first + u] * w[:, u : u + 1] - positive
        return 0

    lax.fori_loop(0, (blk + 2 * half) // UNIT, place, 0)

    def spread(b, _):
        first = b * UNIT
        turn = lax.rem(2 * LANES - half - first, LANES)
        kept = pltpu.roll(keep, turn, 1)
        for g in range(groups):
            cols = slice(g * LANES, (g + 1) * LANES)
            sums = tap_block(lambda t: grads[first + t, :, cols], wide, g, count, True)
            sums = [sums[u] * kept[:, u : u + 1] for u in range(UNIT)]
            block = jnp.concatenate(sums, axis=0).astype(jnp.bfloat16)
            placed[pl.ds(pl.multiple_of(first * SUB, UNIT * SUB), UNIT * SUB), cols] = block
        return 0

    lax.fori_loop(0, blk // UNIT, spread, 0)
    natural = jnp.dot(placement(rows, blk, True), placed[...], preferred_element_type=F32)
    natural = natural.astype(jnp.bfloat16)
    score_grad[...] = natural
    far = column_block(frames, scalars[5], ahead.shape[1])
    part = jnp.dot(turn_over(natural), far, preferred_element_type=F32)
    ahead[...] = part[: query_count // 2]
    behind[...] = part[query_count // 2 :]


def column_block(frames, index, width):
    return frames[:, pl.ds(pl.multiple_of(index * width, LANES), width)]


def turn_over(score_grad):
    return score_grad.astype(F32).T.astype(jnp.bfloat16)


def own_kernel(half, scalars, grads, scores, score_grad, frames, own, taps_out, tap_grads):
    blk = grads.shape[0] - 2 * half
    count = 2 * half + 1
    query_count = score_grad.shape[1]
    groups = query_count // LANES
    tap_grads[...] = jnp.zeros_like(tap_grads)

    def correlate(b, _):
        first = half + b * UNIT
        for g in range(groups):
            cols = slice(g * LANES, (g + 1) * LANES)
            left = [grads[first + u, :, cols] for u in range(UNIT)]
            right = [scores[first + t, :, cols] for t in range(UNIT + count - 1)]
            for j in range(count):
                terms = [left[u] * right[u + j] for u in range(UNIT)]
                while len(terms) > 1:
                    terms = [terms[n] + terms[n + 1] for n in range(0, len(terms), 2)]
                tap_grads[j, :, cols] += terms[0]
        return 0

    lax.fori_loop(0, blk // UNIT, correlate, 0)
    parts = jnp.sum(tap_grads[...], axis=1)
    tall = padded_rows_of(count)
    parts = jnp.concatenate([parts, jnp.zeros((tall - count, query_count), F32)], axis=0)
    part_width = own.shape[1]
    for h in range(query_count // part_width):
        taps_out[h * tall : (h + 1) * tall, :] = parts[:, h * part_width : (h + 1) * part_width]
    mine = column_block(frames, scalars[3], part_width)
    own[...] = jnp.dot(turn_over(score_grad[...]), mine, preferred_element_type=F32)


def near_kernel(
    scalars, score_grad, frames, queries, taps_own, taps_far, from_behind, from_ahead, ahead, behind, frame_part
):
    query_count = score_grad.shape[1]
    part_width = ahead.shape[1]
    middle = query_count // 2
    turned = turn_over(score_grad[...])
    part = jnp.dot(turned, column_block(frames, scalars[4], part_width), preferred_element_type=F32)
    ahead[:middle, :] = part[:middle] + from_behind[...]
    ahead[middle:query_count, :] = part[middle:]
    ahead[query_count:, :] = taps_own[...] + taps_far[...]
    part = jnp.dot(turned, column_block(frames, scalars[6], part_width), preferred_element_type=F32)
    behind[:middle, :] = part[:middle]
    behind[middle:query_count, :] = part[middle:] + from_ahead[...]
    frame_part[...] = jnp.dot(score_grad[...], queries[...], preferred_element_type=F32)


def sum_kernel(own, taps_own, from_behind, from_ahead, taps_far, chunks):
    tms, padded_rows, _ = chunks.shape
    query_count = own.shape[0]
    chunk_rows = query_count // tms
    tap_rows = padded_rows - chunk_rows
    for z in range(tms):
        rows = slice(z * chunk_rows, (z + 1) * chunk_rows)
        chunks[z, :chunk_rows, :] = own[rows, :] + from_behind[rows, :] + from_ahead[rows, :]
        if z * tap_rows < taps_own.shape[0]:
            rows = slice(z * tap_rows, (z + 1) * tap_rows)
            late = slice(query_count + z * tap_rows, query_count + (z + 1) * tap_rows)
            chunks[z, chunk_rows:, :] = taps_own[rows, :] + taps_far[rows, :] + from_behind[late, :]
        else:
            chunks[z, chunk_rows:, :] = jnp.zeros((tap_rows, own.shape[1]), F32)


def padded_rows_of(count):
    return (count + UNIT - 1) // UNIT * UNIT


def per_device(frames, queries, kernel, labels, lengths):
    frame_rows = frames[0]
    rows, width = frame_rows.shape
    query_count = queries.shape[0]
    count = kernel.shape[0]
    half = count // 2
    rim = 2 * half
    blk = rows // SUB
    scale = 10.0 / math.sqrt(width)
    recs, tms, blocks = lax.axis_size("rec"), lax.axis_size("tm"), lax.axis_size("query")
    rec = lax.axis_index("rec")
    ring = [(rec + step) % recs for step in range(4)]
    scalars = jnp.stack(
        [lax.axis_index("tm") * rows, lengths[0], lax.axis_index("query") * query_count] + ring
    ).astype(jnp.int32)
    smem = pl.BlockSpec(memory_space=pltpu.SMEM)

    edge = jax.ShapeDtypeStruct((rim + UNIT, width), F32)
    last, first = pl.pallas_call(
        lambda *refs: edge_kernel(half, *refs),
        out_shape=[edge, edge],
        grid=(1,),
        in_specs=[
            pl.BlockSpec((rim, width), lambda i: (rows // rim - 1, 0)),
            pl.BlockSpec((rim, width), lambda i: (0, 0)),
            pl.BlockSpec(labels.shape, lambda i: (0, 0)),
        ],
        out_specs=[pl.BlockSpec(edge.shape, lambda i: (0, 0))] * 2,
        compiler_params=params(8),
        cost_estimate=cost(rim * width, 1 << 19),
    )(frame_rows, frame_rows, labels)
    up = [(i, i + 1) for i in range(tms - 1)]
    down = [(j, i) for i, j in up]
    before = lax.ppermute(last, "tm", up)
    after = lax.ppermute(first, "tm", down)
    steps = 4
    main = pl.pallas_call(
        lambda *refs: score_kernel(scale, steps, *refs),
        out_shape=jax.ShapeDtypeStruct((rows, query_count), F32),
        grid=(steps,),
        in_specs=[
            smem,
            pl.BlockSpec((rows, width // steps), lambda k: (0, k)),
            pl.BlockSpec((query_count, width // steps), lambda k: (0, k)),
        ],
        out_specs=pl.BlockSpec((rows, query_count), lambda k: (0, 0)),
        scratch_shapes=[VMEM((rows, rows), jnp.bfloat16)],
        compiler_params=params(16),
        cost_estimate=cost(2 * rows * width * (rows + query_count), 3 << 20),
    )(scalars, frame_rows, queries)
    main = main.reshape(blk, SUB, query_count)
    scores, powers, stats, tile = pl.pallas_call(
        lambda *refs: smooth_kernel(scale, half, *refs),
        out_shape=[
            jax.ShapeDtypeStruct((blk + 2 * rim, SUB, query_count), F32),
            jax.ShapeDtypeStruct((blk + rim, SUB, query_count), F32),
            jax.ShapeDtypeStruct((2, SUB, LANES), F32),
            jax.ShapeDtypeStruct((SUB, LANES), F32),
        ],
        in_specs=[smem] + whole_spec(6),
        out_specs=whole_spec(4),
        scratch_shapes=[VMEM((count, SUB, query_count), F32)],
        compiler_params=params(12),
        cost_estimate=cost(4 * rows * query_count * count, 6 << 20),
    )(scalars, main, before, after, labels, queries, kernel)
    others = lax.all_to_all(jnp.broadcast_to(stats[None], (blocks,) + stats.shape), "query", 0, 0)
    chunk_rows = query_count // tms
    part_width = width // recs
    middle = query_count // 2
    grads, score_grad, far_a, far_b = pl.pallas_call(
        lambda *refs: grad_kernel(half, *refs),
        out_shape=[
            jax.ShapeDtypeStruct((blk + rim, SUB, query_count), F32),
            jax.ShapeDtypeStruct((rows, query_count), jnp.bfloat16),
            jax.ShapeDtypeStruct((middle, part_width), F32),
            jax.ShapeDtypeStruct((query_count - middle, part_width), F32),
        ],
        in_specs=[smem] + whole_spec(6),
        out_specs=whole_spec(4),
        scratch_shapes=[
            VMEM((count, SUB, query_count), F32),
            VMEM((rows, query_count), jnp.bfloat16),
        ],
        compiler_params=params(16),
        cost_estimate=cost(2 * rows * query_count * (width + 2 * count), 8 << 20),
    )(scalars, powers, stats, others, tile, frame_rows, kernel)
    onward = [(i, (i + 1) % recs) for i in range(recs)]
    back = [(j, i) for i, j in onward]
    far_a = lax.ppermute(far_a, "rec", onward)
    far_b = lax.ppermute(far_b, "rec", back)
    halves = query_count // part_width
    tap_rows = halves * padded_rows_of(count)
    own, taps_own = pl.pallas_call(
        lambda *refs: own_kernel(half, *refs),
        out_shape=[
            jax.ShapeDtypeStruct((query_count, part_width), F32),
            jax.ShapeDtypeStruct((tap_rows, part_width), F32),
        ],
        in_specs=[smem] + whole_spec(4),
        out_specs=whole_spec(2),
        scratch_shapes=[VMEM((count, SUB, query_count), F32)],
        compiler_params=params(16),
        cost_estimate=cost(4 * rows * query_count * (width + 2 * count), 16 << 20),
    )(scalars, grads, scores, score_grad, frame_rows)
    across = [(i, (i + 2) % recs) for i in range(recs)]
    taps_far = lax.ppermute(taps_own, "rec", across)
    near_a, near_b, frame_part = pl.pallas_call(
        near_kernel,
        out_shape=[
            jax.ShapeDtypeStruct((query_count + tap_rows, part_width), F32),
            jax.ShapeDtypeStruct((query_count, part_width), F32),
            jax.ShapeDtypeStruct((rows, width), F32),
        ],
        in_specs=[smem] + whole_spec(7),
        out_specs=whole_spec(3),
        compiler_params=params(12),
        cost_estimate=cost(rows * query_count * width, 4 << 20),
    )(scalars, score_grad, frame_rows, queries, taps_own, taps_far, far_a, far_b)
    near_a = lax.ppermute(near_a, "rec", onward)
    near_b = lax.ppermute(near_b, "rec", back)
    near_a, near_b, frame_part = lax.optimization_barrier((near_a, near_b, frame_part))
    frame_sum = lax.psum_scatter(frame_part, "query", scatter_dimension=1, tiled=True)
    chunks = pl.pallas_call(
        sum_kernel,
        out_shape=jax.ShapeDtypeStruct((tms, chunk_rows + UNIT, part_width), F32),
        in_specs=whole_spec(5),
        out_specs=pl.BlockSpec(memory_space=VMEM),
        compiler_params=params(8),
        cost_estimate=cost(4 * query_count * part_width, 4 << 20),
    )(own, taps_own, near_a, near_b, taps_far)
    chunk = jnp.sum(lax.all_to_all(chunks, "tm", 0, 0), axis=0)
    frame_sum, chunk = lax.optimization_barrier((frame_sum, chunk))
    whole = lax.all_gather(chunk, "tm")
    query_sum = whole[:, :chunk_rows].reshape(query_count, part_width)
    tap_sum = whole[: tap_rows // UNIT, chunk_rows:].reshape(halves, tap_rows // halves, part_width)
    tap_sum = jnp.concatenate([tap_sum[h, :count] for h in range(halves)], axis=1)
    grad_frames = (frame_sum * scale).astype(jnp.bfloat16)[None]
    grad_queries = (query_sum * scale).astype(jnp.bfloat16)
    return (grad_frames, grad_queries, tap_sum)


def solution(mesh):
    in_specs = (P("rec", "tm", None), P("query", None), P(None, "query"), P("rec", "tm"), P("rec"))
    out_specs = (P("rec", "tm", "query"), P("query", "rec"), P(None, "query"))
    return jax.shard_map(
        per_device, mesh=mesh, in_specs=in_specs, out_specs=out_specs, check_vma=False
    )
```

```python
import math

import jax
import jax.numpy as jnp
from jax import lax
from jax.experimental import pallas as pl
from jax.experimental.pallas import tpu as pltpu
from jax.sharding import PartitionSpec as P

SUB = 8
LANES = 128
VMEM = pltpu.VMEM
F32 = jnp.float32
UNIT = 8


def whole_spec(count):
    return [pl.BlockSpec(memory_space=VMEM)] * count


def params(mib):
    return pltpu.CompilerParams(vmem_limit_bytes=mib << 20)


def cost(flops, bytes_accessed):
    return pl.CostEstimate(flops=flops, bytes_accessed=bytes_accessed, transcendentals=0)


def placement(rows, blk, flipped=False):
    m = lax.broadcasted_iota(jnp.int32, (rows, rows), 1 if flipped else 0)
    f = lax.broadcasted_iota(jnp.int32, (rows, rows), 0 if flipped else 1)
    return jnp.where(f == (m & (SUB - 1)) * blk + m // SUB, 1.0, 0.0).astype(jnp.bfloat16)


def dot_t(a, b):
    return lax.dot_general(a, b, (((1,), (1,)), ((), ())), preferred_element_type=F32)


def edge_kernel(half, last, first, labels, up, down):
    rim = 2 * half
    up[:rim, :] = last[...].astype(F32)
    down[:rim, :] = first[...].astype(F32)
    width = labels.shape[1]
    tail = labels[:, width - LANES :].astype(F32)
    up[rim:, :LANES] = jnp.broadcast_to(pltpu.roll(tail, half, 1), (UNIT, LANES))
    down[rim:, :LANES] = jnp.broadcast_to(labels[:, :LANES].astype(F32), (UNIT, LANES))


def score_kernel(scale, steps, scalars, frames, queries, out, place):
    rows = frames.shape[0]
    blk = rows // SUB
    step = pl.program_id(0)

    @pl.when(step == 0)
    def _():
        place[...] = placement(rows, blk)

    placed = jnp.dot(place[...], frames[...], preferred_element_type=F32).astype(jnp.bfloat16)
    term = dot_t(placed, queries[...])

    @pl.when(step == 0)
    def _():
        out[...] = term

    @pl.when(step > 0)
    def _():
        out[...] += term

    @pl.when(step == steps - 1)
    def _():
        m = lax.broadcasted_iota(jnp.int32, (rows, 1), 0)
        frame = scalars[0] + (m & (SUB - 1)) * blk + m // SUB
        out[...] = jnp.where(frame < scalars[1], out[...] * scale, 0.0)


def label_tile(half, blk, labels, before, after):
    rim = 2 * half
    sub = lax.broadcasted_iota(jnp.int32, (SUB, LANES), 0)
    lane = lax.broadcasted_iota(jnp.int32, (SUB, LANES), 1)
    base = jnp.zeros((SUB, LANES), F32)
    for s in range(SUB):
        at = s * blk
        row = labels[:, at // LANES * LANES : at // LANES * LANES + LANES].astype(F32)
        row = jnp.broadcast_to(row, (SUB, LANES))
        if at % LANES:
            row = pltpu.roll(row, LANES - at % LANES, 1)
        base = jnp.where(sub == s, row, base)
    low = pltpu.roll(pltpu.roll(base, LANES - blk + half, 1), 1, 0)
    low = jnp.where(sub == 0, before[rim:, :LANES], low)
    high = pltpu.roll(pltpu.roll(base, half + blk, 1), SUB - 1, 0)
    high = jnp.where(sub == SUB - 1, pltpu.roll(after[rim:, :LANES], half + blk, 1), high)
    tile = jnp.where(lane < half, low, pltpu.roll(base, half, 1))
    return jnp.where(lane >= half + blk, high, tile)


def broadcast_taps(taps, wide, count):
    for j in range(count):
        wide[j] = jnp.broadcast_to(taps[j : j + 1, :], wide.shape[1:])


def tap_block(load, wide, g, count, flipped):
    sums = [None] * UNIT
    rows = [load(t) for t in range(UNIT + count - 1)]
    for j in range(count):
        tap = wide[count - 1 - j if flipped else j, :, g * LANES : (g + 1) * LANES]
        for u in range(UNIT):
            term = tap * rows[u + j]
            sums[u] = term if sums[u] is None else sums[u] + term
    return sums


def smooth_kernel(
    scale, half, scalars, main, before, after, labels, queries, taps, scores, powers, stats, tile, wide
):
    blk = main.shape[0]
    count = 2 * half + 1
    groups = queries.shape[0] // LANES
    rim = 2 * half
    broadcast_taps(taps, wide, count)
    tile[...] = label_tile(half, blk, labels, before, after)
    rim_frames = jnp.concatenate([before[:rim, :], after[:rim, :]], axis=0).astype(jnp.bfloat16)
    k = lax.broadcasted_iota(jnp.int32, (2 * rim, 1), 0)
    frame = scalars[0] + jnp.where(k < rim, k - rim, blk * SUB + k - rim)
    rim_scores = jnp.where(
        (frame >= 0) & (frame < scalars[1]), dot_t(rim_frames, queries[...]) * scale, 0.0
    )
    sub = lax.broadcasted_iota(jnp.int32, main.shape[1:], 0)
    scores[rim : rim + blk] = main[...]
    for t in range(rim):
        low = pltpu.roll(main[blk - rim + t], 1, 0)
        scores[t] = jnp.where(sub == 0, rim_scores[t : t + 1, :], low)
        high = pltpu.roll(main[t], SUB - 1, 0)
        scores[rim + blk + t] = jnp.where(sub == SUB - 1, rim_scores[rim + t : rim + t + 1, :], high)
    lane = lax.broadcasted_iota(jnp.int32, (SUB, LANES), 1)

    def step(b, carry):
        tops, totals = carry
        first = b * UNIT
        tiles = []
        for g in range(groups):
            cols = slice(g * LANES, (g + 1) * LANES)
            tiles.append(tap_block(lambda t: scores[first + t, :, cols], wide, g, count, False))
        for u in range(UNIT):
            mine = [tiles[g][u] for g in range(groups)]
            peak = mine[0]
            for tile in mine[1:]:
                peak = jnp.maximum(peak, tile)
            top = jnp.max(peak, axis=1, keepdims=True)
            total = None
            for g in range(groups):
                e = jnp.exp(mine[g] - top)
                powers[first + u, :, g * LANES : (g + 1) * LANES] = e
                total = e if total is None else total + e
            total = jnp.sum(total, axis=1, keepdims=True)
            here = lane == first + u
            tops = jnp.where(here, top, tops)
            totals = jnp.where(here, total, totals)
        return tops, totals

    zero = jnp.zeros((SUB, LANES), F32)
    tops, totals = lax.fori_loop(0, (blk + rim) // UNIT, step, (zero, zero))
    stats[0] = tops
    stats[1] = totals


def grad_kernel(
    half, scalars, powers, scores, mine, others, labels, frames, queries, taps,
    score_grad, ahead, behind, keep_frames, cross_frames, wide, grads, tap_grads, placed, frame_part,
):
    blk = powers.shape[0] - 2 * half
    rows = blk * SUB
    count = 2 * half + 1
    query_count = taps.shape[1]
    groups = query_count // LANES
    broadcast_taps(taps, wide, count)
    tops = others[:, 0]
    top = jnp.max(tops, axis=0)
    total = jnp.sum(others[:, 1] * jnp.exp(tops - top[None]), axis=0)
    lane = lax.broadcasted_iota(jnp.int32, (SUB, LANES), 1)
    frame = scalars[0] + lax.broadcasted_iota(jnp.int32, (SUB, LANES), 0) * blk + lane - half
    valid = (frame >= 0) & (frame < scalars[1]) & (lane < blk + 2 * half)
    weight = jnp.where(valid, jnp.exp(mine[0] - top) / total, 0.0)
    label = jnp.where(valid, labels[...] - scalars[2].astype(F32), -1.0)
    keep = jnp.where(valid, 1.0, 0.0)
    ids = lax.broadcasted_iota(jnp.int32, (SUB, query_count), 1).astype(F32)

    def place(b, _):
        first = b * UNIT
        turn = lax.rem(LANES - first, LANES)
        w = pltpu.roll(weight, turn, 1)
        l = pltpu.roll(label, turn, 1)
        for u in range(UNIT):
            positive = jnp.where(ids == l[:, u : u + 1], 1.0, 0.0)
            grads[first + u] = powers[first + u] * w[:, u : u + 1] - positive
        return 0

    lax.fori_loop(0, (blk + 2 * half) // UNIT, place, 0)

    def spread(b, _):
        first = b * UNIT
        turn = lax.rem(2 * LANES - half - first, LANES)
        kept = pltpu.roll(keep, turn, 1)
        for g in range(groups):
            cols = slice(g * LANES, (g + 1) * LANES)
            sums = tap_block(lambda t: grads[first + t, :, cols], wide, g, count, True)
            sums = [sums[u] * kept[:, u : u + 1] for u in range(UNIT)]
            block = jnp.concatenate(sums, axis=0).astype(jnp.bfloat16)
            placed[pl.ds(pl.multiple_of(first * SUB, UNIT * SUB), UNIT * SUB), cols] = block
        return 0

    lax.fori_loop(0, blk // UNIT, spread, 0)
    tap_grads[...] = jnp.zeros_like(tap_grads)

    def correlate(b, _):
        first = half + b * UNIT
        for g in range(groups):
            cols = slice(g * LANES, (g + 1) * LANES)
            left = [grads[first + u, :, cols] for u in range(UNIT)]
            right = [scores[first + t, :, cols] for t in range(UNIT + count - 1)]
            for j in range(count):
                terms = [left[u] * right[u + j] for u in range(UNIT)]
                while len(terms) > 1:
                    terms = [terms[n] + terms[n + 1] for n in range(0, len(terms), 2)]
                tap_grads[j, :, cols] += terms[0]
        return 0

    lax.fori_loop(0, blk // UNIT, correlate, 0)
    parts = jnp.sum(tap_grads[...], axis=1)
    tall = padded_rows_of(count)
    parts = jnp.concatenate([parts, jnp.zeros((tall - count, query_count), F32)], axis=0)
    natural = jnp.dot(placement(rows, blk, True), placed[...], preferred_element_type=F32)
    natural = natural.astype(jnp.bfloat16)
    score_grad[...] = natural
    part_width = ahead.shape[1]
    middle = query_count // 2
    far = column_block(frames, scalars[5], part_width)
    part = jnp.dot(turn_over(natural), far, preferred_element_type=F32)
    ahead[:middle, :] = part[:middle]
    behind[:middle, :] = part[middle:]
    for h in range(query_count // part_width):
        block = parts[:, h * part_width : (h + 1) * part_width]
        ahead[middle + h * tall : middle + (h + 1) * tall, :] = block
        behind[middle + h * tall : middle + (h + 1) * tall, :] = block
    frame_part[...] = jnp.dot(natural, queries[...], preferred_element_type=F32)
    chips, _, out_width = keep_frames.shape
    for k in range(chips):
        keep_frames[k] = column_block(frame_part, scalars[7 + k], out_width)
        cross_frames[k] = column_block(frame_part, scalars[7 + chips + k], out_width)


def column_block(frames, index, width):
    return frames[:, pl.ds(pl.multiple_of(index * width, LANES), width)]


def turn_over(score_grad):
    return score_grad.astype(F32).T.astype(jnp.bfloat16)


def near_kernel(scalars, score_grad, frames, own, ahead, behind):
    turned = turn_over(score_grad[...])
    for index, out in ((3, own), (4, ahead), (6, behind)):
        block = column_block(frames, scalars[index], out.shape[1])
        out[...] = jnp.dot(turned, block, preferred_element_type=F32)


def join_kernel(ahead_in, behind_in, from_behind, from_ahead, keep, crossed, ahead, behind, *frame_out):
    query_count = ahead_in.shape[0]
    middle = query_count // 2
    ahead[:middle, :] = ahead_in[:middle, :] + from_behind[:middle, :]
    ahead[middle:query_count, :] = ahead_in[middle:, :]
    ahead[query_count:, :] = from_behind[middle:, :]
    behind[:middle, :] = behind_in[:middle, :]
    behind[middle:, :] = behind_in[middle:, :] + from_ahead[:middle, :]
    for k, out in enumerate(frame_out):
        out[...] = keep[k] + crossed[k]


def sum_kernel(own, taps, taps_behind, taps_ahead, from_behind, from_ahead, chunks):
    tms, padded_rows, _ = chunks.shape
    query_count = own.shape[0]
    middle = query_count // 2
    chunk_rows = query_count // tms
    tap_rows = padded_rows - chunk_rows
    for z in range(tms):
        rows = slice(z * chunk_rows, (z + 1) * chunk_rows)
        chunks[z, :chunk_rows, :] = own[rows, :] + from_behind[rows, :] + from_ahead[rows, :]
        if z * tap_rows < from_behind.shape[0] - query_count:
            rows = slice(middle + z * tap_rows, middle + (z + 1) * tap_rows)
            late = slice(query_count + z * tap_rows, query_count + (z + 1) * tap_rows)
            chunks[z, chunk_rows:, :] = (
                taps[rows, :] + taps_behind[rows, :] + taps_ahead[rows, :] + from_behind[late, :]
            )
        else:
            chunks[z, chunk_rows:, :] = jnp.zeros((tap_rows, own.shape[1]), F32)


def padded_rows_of(count):
    return (count + UNIT - 1) // UNIT * UNIT


def per_device(frames, queries, kernel, labels, lengths):
    frame_rows = frames[0]
    rows, width = frame_rows.shape
    query_count = queries.shape[0]
    count = kernel.shape[0]
    half = count // 2
    rim = 2 * half
    blk = rows // SUB
    scale = 10.0 / math.sqrt(width)
    recs, tms, blocks = lax.axis_size("rec"), lax.axis_size("tm"), lax.axis_size("query")
    rec = lax.axis_index("rec")
    ring = [(rec + step) % recs for step in range(4)]
    query_index = lax.axis_index("query")
    chips = blocks // 2
    chip, core = query_index // 2, query_index % 2
    keep_ids = [(chip + k) % chips * 2 + core for k in range(chips)]
    cross_ids = [(chip + k) % chips * 2 + 1 - core for k in range(chips)]
    scalars = jnp.stack(
        [lax.axis_index("tm") * rows, lengths[0], query_index * query_count] + ring + keep_ids + cross_ids
    ).astype(jnp.int32)
    smem = pl.BlockSpec(memory_space=pltpu.SMEM)

    edge = jax.ShapeDtypeStruct((rim + UNIT, width), F32)
    last, first = pl.pallas_call(
        lambda *refs: edge_kernel(half, *refs),
        out_shape=[edge, edge],
        grid=(1,),
        in_specs=[
            pl.BlockSpec((rim, width), lambda i: (rows // rim - 1, 0)),
            pl.BlockSpec((rim, width), lambda i: (0, 0)),
            pl.BlockSpec(labels.shape, lambda i: (0, 0)),
        ],
        out_specs=[pl.BlockSpec(edge.shape, lambda i: (0, 0))] * 2,
        compiler_params=params(8),
        cost_estimate=cost(rim * width, 1 << 19),
    )(frame_rows, frame_rows, labels)
    up = [(i, i + 1) for i in range(tms - 1)]
    down = [(j, i) for i, j in up]
    before = lax.ppermute(last, "tm", up)
    after = lax.ppermute(first, "tm", down)
    steps = 4
    main = pl.pallas_call(
        lambda *refs: score_kernel(scale, steps, *refs),
        out_shape=jax.ShapeDtypeStruct((rows, query_count), F32),
        grid=(steps,),
        in_specs=[
            smem,
            pl.BlockSpec((rows, width // steps), lambda k: (0, k)),
            pl.BlockSpec((query_count, width // steps), lambda k: (0, k)),
        ],
        out_specs=pl.BlockSpec((rows, query_count), lambda k: (0, 0)),
        scratch_shapes=[VMEM((rows, rows), jnp.bfloat16)],
        compiler_params=params(16),
        cost_estimate=cost(2 * rows * width * (rows + query_count), 3 << 20),
    )(scalars, frame_rows, queries)
    main = main.reshape(blk, SUB, query_count)
    scores, powers, stats, tile = pl.pallas_call(
        lambda *refs: smooth_kernel(scale, half, *refs),
        out_shape=[
            jax.ShapeDtypeStruct((blk + 2 * rim, SUB, query_count), F32),
            jax.ShapeDtypeStruct((blk + rim, SUB, query_count), F32),
            jax.ShapeDtypeStruct((2, SUB, LANES), F32),
            jax.ShapeDtypeStruct((SUB, LANES), F32),
        ],
        in_specs=[smem] + whole_spec(6),
        out_specs=whole_spec(4),
        scratch_shapes=[VMEM((count, SUB, query_count), F32)],
        compiler_params=params(12),
        cost_estimate=cost(4 * rows * query_count * count, 6 << 20),
    )(scalars, main, before, after, labels, queries, kernel)
    others = lax.all_to_all(jnp.broadcast_to(stats[None], (blocks,) + stats.shape), "query", 0, 0)
    chunk_rows = query_count // tms
    part_width = width // recs
    middle = query_count // 2
    halves = query_count // part_width
    tap_rows = halves * padded_rows_of(count)
    out_width = width // blocks
    step = jax.ShapeDtypeStruct((middle + tap_rows, part_width), F32)
    terms = jax.ShapeDtypeStruct((chips, rows, out_width), F32)
    score_grad, far_a, far_b, keep, cross = pl.pallas_call(
        lambda *refs: grad_kernel(half, *refs),
        out_shape=[jax.ShapeDtypeStruct((rows, query_count), jnp.bfloat16), step, step, terms, terms],
        in_specs=[smem] + whole_spec(8),
        out_specs=whole_spec(5),
        scratch_shapes=[
            VMEM((count, SUB, query_count), F32),
            VMEM((blk + rim, SUB, query_count), F32),
            VMEM((count, SUB, query_count), F32),
            VMEM((rows, query_count), jnp.bfloat16),
            VMEM((rows, width), F32),
        ],
        compiler_params=params(20),
        cost_estimate=cost(2 * rows * query_count * (width + 2 * count), 8 << 20),
    )(scalars, powers, scores, stats, others, tile, frame_rows, queries, kernel)
    onward = [(i, (i + 1) % recs) for i in range(recs)]
    back = [(j, i) for i, j in onward]
    taps_behind = lax.ppermute(far_a, "rec", onward)
    taps_ahead = lax.ppermute(far_b, "rec", back)
    crossed = lax.ppermute(cross, "query", [(i, i ^ 1) for i in range(blocks)])
    near = jax.ShapeDtypeStruct((query_count, part_width), F32)
    own, near_a, near_b = pl.pallas_call(
        near_kernel,
        out_shape=[near, near, near],
        in_specs=[smem] + whole_spec(2),
        out_specs=whole_spec(3),
        compiler_params=params(12),
        cost_estimate=cost(2 * rows * query_count * width, 4 << 20),
    )(scalars, score_grad, frame_rows)
    near_a, near_b, *sends = pl.pallas_call(
        join_kernel,
        out_shape=[jax.ShapeDtypeStruct((query_count + tap_rows, part_width), F32), near]
        + [jax.ShapeDtypeStruct((rows, out_width), F32)] * chips,
        in_specs=whole_spec(6),
        out_specs=whole_spec(2 + chips),
        compiler_params=params(8),
        cost_estimate=cost(rows * width, 4 << 20),
    )(near_a, near_b, taps_behind, taps_ahead, keep, crossed)
    near_a = lax.ppermute(near_a, "rec", onward)
    near_b = lax.ppermute(near_b, "rec", back)
    arrived = [
        lax.ppermute(sends[k], "query", [(i, (i + 2 * k) % blocks) for i in range(blocks)])
        for k in range(1, chips)
    ]
    chunks = pl.pallas_call(
        sum_kernel,
        out_shape=jax.ShapeDtypeStruct((tms, chunk_rows + UNIT, part_width), F32),
        in_specs=whole_spec(6),
        out_specs=pl.BlockSpec(memory_space=VMEM),
        compiler_params=params(8),
        cost_estimate=cost(4 * query_count * part_width, 4 << 20),
    )(own, far_a, taps_behind, taps_ahead, near_a, near_b)
    chunk = jnp.sum(lax.all_to_all(chunks, "tm", 0, 0), axis=0)
    whole = lax.all_gather(chunk, "tm")
    *arrived, whole = lax.optimization_barrier((*arrived, whole))
    frame_sum = sends[0]
    for term in arrived:
        frame_sum = frame_sum + term
    query_sum = whole[:, :chunk_rows].reshape(query_count, part_width)
    tap_sum = whole[: tap_rows // UNIT, chunk_rows:].reshape(halves, tap_rows // halves, part_width)
    tap_sum = jnp.concatenate([tap_sum[h, :count] for h in range(halves)], axis=1)
    grad_frames = (frame_sum * scale).astype(jnp.bfloat16)[None]
    grad_queries = (query_sum * scale).astype(jnp.bfloat16)
    return (grad_frames, grad_queries, tap_sum)


def solution(mesh):
    in_specs = (P("rec", "tm", None), P("query", None), P(None, "query"), P("rec", "tm"), P("rec"))
    out_specs = (P("rec", "tm", "query"), P("query", "rec"), P(None, "query"))
    return jax.shard_map(
        per_device, mesh=mesh, in_specs=in_specs, out_specs=out_specs, check_vma=False
    )
```

```python
import math

import jax
import jax.numpy as jnp
from jax import lax
from jax.experimental import pallas as pl
from jax.experimental.pallas import tpu as pltpu
from jax.sharding import PartitionSpec as P

SUB = 8
LANES = 128
VMEM = pltpu.VMEM
F32 = jnp.float32
UNIT = 8


def whole_spec(count):
    return [pl.BlockSpec(memory_space=VMEM)] * count


def params(mib):
    return pltpu.CompilerParams(vmem_limit_bytes=mib << 20)


def cost(flops, bytes_accessed):
    return pl.CostEstimate(flops=flops, bytes_accessed=bytes_accessed, transcendentals=0)


def placement(rows, blk, flipped=False):
    m = lax.broadcasted_iota(jnp.int32, (rows, rows), 1 if flipped else 0)
    f = lax.broadcasted_iota(jnp.int32, (rows, rows), 0 if flipped else 1)
    return jnp.where(f == (m & (SUB - 1)) * blk + m // SUB, 1.0, 0.0).astype(jnp.bfloat16)


def dot_t(a, b):
    return lax.dot_general(a, b, (((1,), (1,)), ((), ())), preferred_element_type=F32)


def edge_kernel(half, last, first, labels, up, down):
    rim = 2 * half
    up[:rim, :] = last[...].astype(F32)
    down[:rim, :] = first[...].astype(F32)
    width = labels.shape[1]
    tail = labels[:, width - LANES :].astype(F32)
    up[rim:, :LANES] = jnp.broadcast_to(pltpu.roll(tail, half, 1), (UNIT, LANES))
    down[rim:, :LANES] = jnp.broadcast_to(labels[:, :LANES].astype(F32), (UNIT, LANES))


def score_kernel(scale, steps, scalars, frames, queries, out, place):
    rows = frames.shape[0]
    blk = rows // SUB
    step = pl.program_id(0)

    @pl.when(step == 0)
    def _():
        place[...] = placement(rows, blk)

    placed = jnp.dot(place[...], frames[...], preferred_element_type=F32).astype(jnp.bfloat16)
    term = dot_t(placed, queries[...])

    @pl.when(step == 0)
    def _():
        out[...] = term

    @pl.when(step > 0)
    def _():
        out[...] += term

    @pl.when(step == steps - 1)
    def _():
        m = lax.broadcasted_iota(jnp.int32, (rows, 1), 0)
        frame = scalars[0] + (m & (SUB - 1)) * blk + m // SUB
        out[...] = jnp.where(frame < scalars[1], out[...] * scale, 0.0)


def label_tile(half, blk, labels, before, after):
    rim = 2 * half
    sub = lax.broadcasted_iota(jnp.int32, (SUB, LANES), 0)
    lane = lax.broadcasted_iota(jnp.int32, (SUB, LANES), 1)
    base = jnp.zeros((SUB, LANES), F32)
    for s in range(SUB):
        at = s * blk
        row = labels[:, at // LANES * LANES : at // LANES * LANES + LANES].astype(F32)
        row = jnp.broadcast_to(row, (SUB, LANES))
        if at % LANES:
            row = pltpu.roll(row, LANES - at % LANES, 1)
        base = jnp.where(sub == s, row, base)
    low = pltpu.roll(pltpu.roll(base, LANES - blk + half, 1), 1, 0)
    low = jnp.where(sub == 0, before[rim:, :LANES], low)
    high = pltpu.roll(pltpu.roll(base, half + blk, 1), SUB - 1, 0)
    high = jnp.where(sub == SUB - 1, pltpu.roll(after[rim:, :LANES], half + blk, 1), high)
    tile = jnp.where(lane < half, low, pltpu.roll(base, half, 1))
    return jnp.where(lane >= half + blk, high, tile)


def broadcast_taps(taps, wide, count):
    for j in range(count):
        wide[j] = jnp.broadcast_to(taps[j : j + 1, :], wide.shape[1:])


def tap_block(load, wide, g, count, flipped):
    sums = [None] * UNIT
    rows = [load(t) for t in range(UNIT + count - 1)]
    for j in range(count):
        tap = wide[count - 1 - j if flipped else j, :, g * LANES : (g + 1) * LANES]
        for u in range(UNIT):
            term = tap * rows[u + j]
            sums[u] = term if sums[u] is None else sums[u] + term
    return sums


def smooth_kernel(
    scale, half, scalars, main, before, after, labels, queries, taps, scores, powers, stats, tile, wide
):
    blk = main.shape[0]
    count = 2 * half + 1
    groups = queries.shape[0] // LANES
    rim = 2 * half
    broadcast_taps(taps, wide, count)
    tile[...] = label_tile(half, blk, labels, before, after)
    rim_frames = jnp.concatenate([before[:rim, :], after[:rim, :]], axis=0).astype(jnp.bfloat16)
    k = lax.broadcasted_iota(jnp.int32, (2 * rim, 1), 0)
    frame = scalars[0] + jnp.where(k < rim, k - rim, blk * SUB + k - rim)
    rim_scores = jnp.where(
        (frame >= 0) & (frame < scalars[1]), dot_t(rim_frames, queries[...]) * scale, 0.0
    )
    sub = lax.broadcasted_iota(jnp.int32, main.shape[1:], 0)
    scores[rim : rim + blk] = main[...]
    for t in range(rim):
        low = pltpu.roll(main[blk - rim + t], 1, 0)
        scores[t] = jnp.where(sub == 0, rim_scores[t : t + 1, :], low)
        high = pltpu.roll(main[t], SUB - 1, 0)
        scores[rim + blk + t] = jnp.where(sub == SUB - 1, rim_scores[rim + t : rim + t + 1, :], high)
    lane = lax.broadcasted_iota(jnp.int32, (SUB, LANES), 1)

    def step(b, carry):
        tops, totals = carry
        first = b * UNIT
        tiles = []
        for g in range(groups):
            cols = slice(g * LANES, (g + 1) * LANES)
            tiles.append(tap_block(lambda t: scores[first + t, :, cols], wide, g, count, False))
        for u in range(UNIT):
            mine = [tiles[g][u] for g in range(groups)]
            peak = mine[0]
            for tile in mine[1:]:
                peak = jnp.maximum(peak, tile)
            top = jnp.max(peak, axis=1, keepdims=True)
            total = None
            for g in range(groups):
                e = jnp.exp(mine[g] - top)
                powers[first + u, :, g * LANES : (g + 1) * LANES] = e
                total = e if total is None else total + e
            total = jnp.sum(total, axis=1, keepdims=True)
            here = lane == first + u
            tops = jnp.where(here, top, tops)
            totals = jnp.where(here, total, totals)
        return tops, totals

    zero = jnp.zeros((SUB, LANES), F32)
    tops, totals = lax.fori_loop(0, (blk + rim) // UNIT, step, (zero, zero))
    stats[0] = tops
    stats[1] = totals


def grad_kernel(
    half, scalars, powers, scores, mine, others, labels, frames, queries, taps,
    chunks, tap_sums, keep_frames, cross_frames, wide, grads, tap_grads, placed, frame_part,
):
    blk = powers.shape[0] - 2 * half
    rows = blk * SUB
    count = 2 * half + 1
    query_count = taps.shape[1]
    groups = query_count // LANES
    broadcast_taps(taps, wide, count)
    tops = others[:, 0]
    top = jnp.max(tops, axis=0)
    total = jnp.sum(others[:, 1] * jnp.exp(tops - top[None]), axis=0)
    lane = lax.broadcasted_iota(jnp.int32, (SUB, LANES), 1)
    frame = scalars[0] + lax.broadcasted_iota(jnp.int32, (SUB, LANES), 0) * blk + lane - half
    valid = (frame >= 0) & (frame < scalars[1]) & (lane < blk + 2 * half)
    weight = jnp.where(valid, jnp.exp(mine[0] - top) / total, 0.0)
    label = jnp.where(valid, labels[...] - scalars[2].astype(F32), -1.0)
    keep = jnp.where(valid, 1.0, 0.0)
    ids = lax.broadcasted_iota(jnp.int32, (SUB, query_count), 1).astype(F32)

    def place(b, _):
        first = b * UNIT
        turn = lax.rem(LANES - first, LANES)
        w = pltpu.roll(weight, turn, 1)
        l = pltpu.roll(label, turn, 1)
        for u in range(UNIT):
            positive = jnp.where(ids == l[:, u : u + 1], 1.0, 0.0)
            grads[first + u] = powers[first + u] * w[:, u : u + 1] - positive
        return 0

    lax.fori_loop(0, (blk + 2 * half) // UNIT, place, 0)

    def spread(b, _):
        first = b * UNIT
        turn = lax.rem(2 * LANES - half - first, LANES)
        kept = pltpu.roll(keep, turn, 1)
        for g in range(groups):
            cols = slice(g * LANES, (g + 1) * LANES)
            sums = tap_block(lambda t: grads[first + t, :, cols], wide, g, count, True)
            sums = [sums[u] * kept[:, u : u + 1] for u in range(UNIT)]
            block = jnp.concatenate(sums, axis=0).astype(jnp.bfloat16)
            placed[pl.ds(pl.multiple_of(first * SUB, UNIT * SUB), UNIT * SUB), cols] = block
        return 0

    lax.fori_loop(0, blk // UNIT, spread, 0)
    tap_grads[...] = jnp.zeros_like(tap_grads)

    def correlate(b, _):
        first = half + b * UNIT
        for g in range(groups):
            cols = slice(g * LANES, (g + 1) * LANES)
            left = [grads[first + u, :, cols] for u in range(UNIT)]
            right = [scores[first + t, :, cols] for t in range(UNIT + count - 1)]
            for j in range(count):
                terms = [left[u] * right[u + j] for u in range(UNIT)]
                while len(terms) > 1:
                    terms = [terms[n] + terms[n + 1] for n in range(0, len(terms), 2)]
                tap_grads[j, :, cols] += terms[0]
        return 0

    lax.fori_loop(0, blk // UNIT, correlate, 0)
    tap_sums[:count, :] = jnp.sum(tap_grads[...], axis=1)
    tap_sums[count:, :] = jnp.zeros((tap_sums.shape[0] - count, query_count), F32)
    natural = jnp.dot(placement(rows, blk, True), placed[...], preferred_element_type=F32)
    turned = natural.T.astype(jnp.bfloat16)
    natural = natural.astype(jnp.bfloat16)
    recs, part_rows, part_width = chunks.shape
    for r in range(recs):
        chunks[r] = jnp.dot(turned, frames[:, r * part_width : (r + 1) * part_width], preferred_element_type=F32)
    frame_part[...] = jnp.dot(natural, queries[...], preferred_element_type=F32)
    chips, _, out_width = keep_frames.shape
    for k in range(chips):
        keep_frames[k] = column_block(frame_part, scalars[3 + k], out_width)
        cross_frames[k] = column_block(frame_part, scalars[3 + chips + k], out_width)


def column_block(frames, index, width):
    return frames[:, pl.ds(pl.multiple_of(index * width, LANES), width)]


def sum_kernel(arrived, taps_own, taps_far, taps_behind, taps_ahead, chunks, taps):
    tms, padded_rows, part_width = chunks.shape
    tall, query_count = taps.shape
    taps[...] = (taps_own[...] + taps_far[...]) + (taps_behind[...] + taps_ahead[...])
    chunk_rows = query_count // tms
    tap_blocks = tall // UNIT
    for z in range(tms):
        rows = slice(z * chunk_rows, (z + 1) * chunk_rows)
        total = arrived[0, rows, :]
        for r in range(1, arrived.shape[0]):
            total = total + arrived[r, rows, :]
        chunks[z, :chunk_rows, :] = total
        h, t = z // tap_blocks, z % tap_blocks
        if h * part_width < query_count:
            block = taps[t * UNIT : (t + 1) * UNIT, h * part_width : (h + 1) * part_width]
            chunks[z, chunk_rows:, :] = block
        else:
            chunks[z, chunk_rows:, :] = jnp.zeros((UNIT, part_width), F32)


def padded_rows_of(count):
    return (count + UNIT - 1) // UNIT * UNIT


def per_device(frames, queries, kernel, labels, lengths):
    frame_rows = frames[0]
    rows, width = frame_rows.shape
    query_count = queries.shape[0]
    count = kernel.shape[0]
    half = count // 2
    rim = 2 * half
    blk = rows // SUB
    scale = 10.0 / math.sqrt(width)
    recs, tms, blocks = lax.axis_size("rec"), lax.axis_size("tm"), lax.axis_size("query")
    query_index = lax.axis_index("query")
    chips = blocks // 2
    chip, core = query_index // 2, query_index % 2
    keep_ids = [(chip + k) % chips * 2 + core for k in range(chips)]
    cross_ids = [(chip + k) % chips * 2 + 1 - core for k in range(chips)]
    scalars = jnp.stack(
        [lax.axis_index("tm") * rows, lengths[0], query_index * query_count] + keep_ids + cross_ids
    ).astype(jnp.int32)
    smem = pl.BlockSpec(memory_space=pltpu.SMEM)

    edge = jax.ShapeDtypeStruct((rim + UNIT, width), F32)
    last, first = pl.pallas_call(
        lambda *refs: edge_kernel(half, *refs),
        out_shape=[edge, edge],
        grid=(1,),
        in_specs=[
            pl.BlockSpec((rim, width), lambda i: (rows // rim - 1, 0)),
            pl.BlockSpec((rim, width), lambda i: (0, 0)),
            pl.BlockSpec(labels.shape, lambda i: (0, 0)),
        ],
        out_specs=[pl.BlockSpec(edge.shape, lambda i: (0, 0))] * 2,
        compiler_params=params(8),
        cost_estimate=cost(rim * width, 1 << 19),
    )(frame_rows, frame_rows, labels)
    up = [(i, i + 1) for i in range(tms - 1)]
    down = [(j, i) for i, j in up]
    before = lax.ppermute(last, "tm", up)
    after = lax.ppermute(first, "tm", down)
    steps = 4
    main = pl.pallas_call(
        lambda *refs: score_kernel(scale, steps, *refs),
        out_shape=jax.ShapeDtypeStruct((rows, query_count), F32),
        grid=(steps,),
        in_specs=[
            smem,
            pl.BlockSpec((rows, width // steps), lambda k: (0, k)),
            pl.BlockSpec((query_count, width // steps), lambda k: (0, k)),
        ],
        out_specs=pl.BlockSpec((rows, query_count), lambda k: (0, 0)),
        scratch_shapes=[VMEM((rows, rows), jnp.bfloat16)],
        compiler_params=params(16),
        cost_estimate=cost(2 * rows * width * (rows + query_count), 3 << 20),
    )(scalars, frame_rows, queries)
    main = main.reshape(blk, SUB, query_count)
    scores, powers, stats, tile = pl.pallas_call(
        lambda *refs: smooth_kernel(scale, half, *refs),
        out_shape=[
            jax.ShapeDtypeStruct((blk + 2 * rim, SUB, query_count), F32),
            jax.ShapeDtypeStruct((blk + rim, SUB, query_count), F32),
            jax.ShapeDtypeStruct((2, SUB, LANES), F32),
            jax.ShapeDtypeStruct((SUB, LANES), F32),
        ],
        in_specs=[smem] + whole_spec(6),
        out_specs=whole_spec(4),
        scratch_shapes=[VMEM((count, SUB, query_count), F32)],
        compiler_params=params(12),
        cost_estimate=cost(4 * rows * query_count * count, 6 << 20),
    )(scalars, main, before, after, labels, queries, kernel)
    others = lax.all_to_all(jnp.broadcast_to(stats[None], (blocks,) + stats.shape), "query", 0, 0)
    chunk_rows = query_count // tms
    part_width = width // recs
    out_width = width // blocks
    terms = jax.ShapeDtypeStruct((chips, rows, out_width), F32)
    parts, tap_sum, keep, cross = pl.pallas_call(
        lambda *refs: grad_kernel(half, *refs),
        out_shape=[
            jax.ShapeDtypeStruct((recs, query_count, part_width), F32),
            jax.ShapeDtypeStruct((padded_rows_of(count), query_count), F32),
            terms,
            terms,
        ],
        in_specs=[smem] + whole_spec(8),
        out_specs=whole_spec(4),
        scratch_shapes=[
            VMEM((count, SUB, query_count), F32),
            VMEM((blk + rim, SUB, query_count), F32),
            VMEM((count, SUB, query_count), F32),
            VMEM((rows, query_count), jnp.bfloat16),
            VMEM((rows, width), F32),
        ],
        compiler_params=params(20),
        cost_estimate=cost(2 * rows * query_count * (width + 2 * count), 8 << 20),
    )(scalars, powers, scores, stats, others, tile, frame_rows, queries, kernel)
    parts = lax.all_to_all(parts, "rec", 0, 0)
    crossed = lax.ppermute(cross, "query", [(i, i ^ 1) for i in range(blocks)])
    far, behind, ahead = [
        lax.ppermute(tap_sum, "rec", [(i, (i + k) % recs) for i in range(recs)]) for k in (2, 1, 3)
    ]
    parts, keep, crossed = lax.optimization_barrier((parts, keep, crossed))
    chunks = pl.pallas_call(
        sum_kernel,
        out_shape=jax.ShapeDtypeStruct((tms, chunk_rows + UNIT, part_width), F32),
        in_specs=whole_spec(5),
        out_specs=pl.BlockSpec(memory_space=VMEM),
        scratch_shapes=[VMEM((padded_rows_of(count), query_count), F32)],
        compiler_params=params(8),
        cost_estimate=cost(4 * query_count * part_width, 4 << 20),
    )(parts, tap_sum, far, behind, ahead)
    chunk = jnp.sum(lax.all_to_all(chunks, "tm", 0, 0), axis=0)
    sends = [keep[k] + crossed[k] for k in range(chips)]
    frame_sum = sends[0]
    for k in range(1, chips):
        frame_sum = frame_sum + lax.ppermute(sends[k], "query", [(i, (i + 2 * k) % blocks) for i in range(blocks)])
    chunk, frame_sum = lax.optimization_barrier((chunk, frame_sum))
    whole = lax.all_gather(chunk, "tm")
    query_sum = whole[:, :chunk_rows].reshape(query_count, part_width)
    halves = query_count // part_width
    tall = padded_rows_of(count)
    tap_sum = whole[: halves * tall // UNIT, chunk_rows:].reshape(halves, tall, part_width)
    tap_sum = jnp.concatenate([tap_sum[h, :count] for h in range(halves)], axis=1)
    grad_frames = (frame_sum * scale).astype(jnp.bfloat16)[None]
    grad_queries = (query_sum * scale).astype(jnp.bfloat16)
    return (grad_frames, grad_queries, tap_sum)


def solution(mesh):
    in_specs = (P("rec", "tm", None), P("query", None), P(None, "query"), P("rec", "tm"), P("rec"))
    out_specs = (P("rec", "tm", "query"), P("query", "rec"), P(None, "query"))
    return jax.shard_map(
        per_device, mesh=mesh, in_specs=in_specs, out_specs=out_specs, check_vma=False
    )
```

```python
import math

import jax
import jax.numpy as jnp
from jax import lax
from jax.experimental import pallas as pl
from jax.experimental.pallas import tpu as pltpu
from jax.sharding import PartitionSpec as P

SUB = 8
LANES = 128
VMEM = pltpu.VMEM
F32 = jnp.float32
UNIT = 8


def whole_spec(count):
    return [pl.BlockSpec(memory_space=VMEM)] * count


def params(mib):
    return pltpu.CompilerParams(vmem_limit_bytes=mib << 20)


def cost(flops, bytes_accessed):
    return pl.CostEstimate(flops=flops, bytes_accessed=bytes_accessed, transcendentals=0)


def placement(rows, blk, flipped=False):
    m = lax.broadcasted_iota(jnp.int32, (rows, rows), 1 if flipped else 0)
    f = lax.broadcasted_iota(jnp.int32, (rows, rows), 0 if flipped else 1)
    return jnp.where(f == (m & (SUB - 1)) * blk + m // SUB, 1.0, 0.0).astype(jnp.bfloat16)


def dot_t(a, b):
    return lax.dot_general(a, b, (((1,), (1,)), ((), ())), preferred_element_type=F32)


def edge_kernel(half, last, first, labels, up, down):
    rim = 2 * half
    up[:rim, :] = last[...].astype(F32)
    down[:rim, :] = first[...].astype(F32)
    width = labels.shape[1]
    tail = labels[:, width - LANES :].astype(F32)
    up[rim:, :LANES] = jnp.broadcast_to(pltpu.roll(tail, half, 1), (UNIT, LANES))
    down[rim:, :LANES] = jnp.broadcast_to(labels[:, :LANES].astype(F32), (UNIT, LANES))


def score_kernel(scale, steps, scalars, frames, queries, out, place):
    rows = frames.shape[0]
    blk = rows // SUB
    step = pl.program_id(0)

    @pl.when(step == 0)
    def _():
        place[...] = placement(rows, blk)

    placed = jnp.dot(place[...], frames[...], preferred_element_type=F32).astype(jnp.bfloat16)
    term = dot_t(placed, queries[...])

    @pl.when(step == 0)
    def _():
        out[...] = term

    @pl.when(step > 0)
    def _():
        out[...] += term

    @pl.when(step == steps - 1)
    def _():
        m = lax.broadcasted_iota(jnp.int32, (rows, 1), 0)
        frame = scalars[0] + (m & (SUB - 1)) * blk + m // SUB
        out[...] = jnp.where(frame < scalars[1], out[...] * scale, 0.0)


def label_tile(half, blk, labels, before, after):
    rim = 2 * half
    sub = lax.broadcasted_iota(jnp.int32, (SUB, LANES), 0)
    lane = lax.broadcasted_iota(jnp.int32, (SUB, LANES), 1)
    base = jnp.zeros((SUB, LANES), F32)
    for s in range(SUB):
        at = s * blk
        row = labels[:, at // LANES * LANES : at // LANES * LANES + LANES].astype(F32)
        row = jnp.broadcast_to(row, (SUB, LANES))
        if at % LANES:
            row = pltpu.roll(row, LANES - at % LANES, 1)
        base = jnp.where(sub == s, row, base)
    low = pltpu.roll(pltpu.roll(base, LANES - blk + half, 1), 1, 0)
    low = jnp.where(sub == 0, before[rim:, :LANES], low)
    high = pltpu.roll(pltpu.roll(base, half + blk, 1), SUB - 1, 0)
    high = jnp.where(sub == SUB - 1, pltpu.roll(after[rim:, :LANES], half + blk, 1), high)
    tile = jnp.where(lane < half, low, pltpu.roll(base, half, 1))
    return jnp.where(lane >= half + blk, high, tile)


def broadcast_taps(taps, wide, count):
    for j in range(count):
        wide[j] = jnp.broadcast_to(taps[j : j + 1, :], wide.shape[1:])


def tap_block(load, wide, g, count, flipped):
    sums = [None] * UNIT
    rows = [load(t) for t in range(UNIT + count - 1)]
    for j in range(count):
        tap = wide[count - 1 - j if flipped else j, :, g * LANES : (g + 1) * LANES]
        for u in range(UNIT):
            term = tap * rows[u + j]
            sums[u] = term if sums[u] is None else sums[u] + term
    return sums


def smooth_kernel(
    scale, half, scalars, main, before, after, labels, queries, taps, scores_out, powers, stats, tile, wide, scores, sem
):
    blk = main.shape[0]
    count = 2 * half + 1
    groups = queries.shape[0] // LANES
    rim = 2 * half
    broadcast_taps(taps, wide, count)
    tile[...] = label_tile(half, blk, labels, before, after)
    rim_frames = jnp.concatenate([before[:rim, :], after[:rim, :]], axis=0).astype(jnp.bfloat16)
    k = lax.broadcasted_iota(jnp.int32, (2 * rim, 1), 0)
    frame = scalars[0] + jnp.where(k < rim, k - rim, blk * SUB + k - rim)
    rim_scores = jnp.where(
        (frame >= 0) & (frame < scalars[1]), dot_t(rim_frames, queries[...]) * scale, 0.0
    )
    sub = lax.broadcasted_iota(jnp.int32, main.shape[1:], 0)
    scores[rim : rim + blk] = main[...]
    for t in range(rim):
        low = pltpu.roll(main[blk - rim + t], 1, 0)
        scores[t] = jnp.where(sub == 0, rim_scores[t : t + 1, :], low)
        high = pltpu.roll(main[t], SUB - 1, 0)
        scores[rim + blk + t] = jnp.where(sub == SUB - 1, rim_scores[rim + t : rim + t + 1, :], high)
    copy = pltpu.make_async_copy(scores, scores_out, sem)
    copy.start()
    lane = lax.broadcasted_iota(jnp.int32, (SUB, LANES), 1)

    def step(b, carry):
        tops, totals = carry
        first = b * UNIT
        tiles = []
        for g in range(groups):
            cols = slice(g * LANES, (g + 1) * LANES)
            tiles.append(tap_block(lambda t: scores[first + t, :, cols], wide, g, count, False))
        for u in range(UNIT):
            mine = [tiles[g][u] for g in range(groups)]
            peak = mine[0]
            for tile in mine[1:]:
                peak = jnp.maximum(peak, tile)
            top = jnp.max(peak, axis=1, keepdims=True)
            total = None
            for g in range(groups):
                e = jnp.exp(mine[g] - top)
                powers[first + u, :, g * LANES : (g + 1) * LANES] = e
                total = e if total is None else total + e
            total = jnp.sum(total, axis=1, keepdims=True)
            here = lane == first + u
            tops = jnp.where(here, top, tops)
            totals = jnp.where(here, total, totals)
        return tops, totals

    zero = jnp.zeros((SUB, LANES), F32)
    tops, totals = lax.fori_loop(0, (blk + rim) // UNIT, step, (zero, zero))
    stats[0] = tops
    stats[1] = totals
    copy.wait()


def grad_kernel(
    half, scalars, powers, scores_in, mine, others, labels, frames, queries, taps,
    chunks_out, tap_sums, keep_frames, cross_out, wide, grads, tap_grads, placed, frame_part, chunks, cross_frames, scores, sems,
):
    blk = powers.shape[0] - 2 * half
    rows = blk * SUB
    count = 2 * half + 1
    query_count = taps.shape[1]
    groups = query_count // LANES
    fetch = pltpu.make_async_copy(scores_in, scores, sems.at[sems.shape[0] - 1])
    fetch.start()
    broadcast_taps(taps, wide, count)
    tops = others[:, 0]
    top = jnp.max(tops, axis=0)
    total = jnp.sum(others[:, 1] * jnp.exp(tops - top[None]), axis=0)
    lane = lax.broadcasted_iota(jnp.int32, (SUB, LANES), 1)
    frame = scalars[0] + lax.broadcasted_iota(jnp.int32, (SUB, LANES), 0) * blk + lane - half
    valid = (frame >= 0) & (frame < scalars[1]) & (lane < blk + 2 * half)
    weight = jnp.where(valid, jnp.exp(mine[0] - top) / total, 0.0)
    label = jnp.where(valid, labels[...] - scalars[2].astype(F32), -1.0)
    keep = jnp.where(valid, 1.0, 0.0)
    ids = lax.broadcasted_iota(jnp.int32, (SUB, query_count), 1).astype(F32)

    def place(b, _):
        first = b * UNIT
        turn = lax.rem(LANES - first, LANES)
        w = pltpu.roll(weight, turn, 1)
        l = pltpu.roll(label, turn, 1)
        for u in range(UNIT):
            positive = jnp.where(ids == l[:, u : u + 1], 1.0, 0.0)
            grads[first + u] = powers[first + u] * w[:, u : u + 1] - positive
        return 0

    lax.fori_loop(0, (blk + 2 * half) // UNIT, place, 0)

    def spread(b, _):
        first = b * UNIT
        turn = lax.rem(2 * LANES - half - first, LANES)
        kept = pltpu.roll(keep, turn, 1)
        for g in range(groups):
            cols = slice(g * LANES, (g + 1) * LANES)
            sums = tap_block(lambda t: grads[first + t, :, cols], wide, g, count, True)
            sums = [sums[u] * kept[:, u : u + 1] for u in range(UNIT)]
            block = jnp.concatenate(sums, axis=0).astype(jnp.bfloat16)
            placed[pl.ds(pl.multiple_of(first * SUB, UNIT * SUB), UNIT * SUB), cols] = block
        return 0

    lax.fori_loop(0, blk // UNIT, spread, 0)
    natural = jnp.dot(placement(rows, blk, True), placed[...], preferred_element_type=F32)
    turned = natural.T.astype(jnp.bfloat16)
    natural = natural.astype(jnp.bfloat16)
    recs, part_rows, part_width = chunks.shape
    copies = []
    for r in range(recs):
        chunks[r] = jnp.dot(turned, frames[:, r * part_width : (r + 1) * part_width], preferred_element_type=F32)
        copies.append(pltpu.make_async_copy(chunks.at[r], chunks_out.at[r], sems.at[r]))
        copies[r].start()
    frame_part[...] = jnp.dot(natural, queries[...], preferred_element_type=F32)
    chips, _, out_width = keep_frames.shape
    for k in range(chips):
        keep_frames[k] = column_block(frame_part, scalars[3 + k], out_width)
        cross_frames[k] = column_block(frame_part, scalars[3 + chips + k], out_width)
    copies.append(pltpu.make_async_copy(cross_frames, cross_out, sems.at[recs]))
    copies[recs].start()
    tap_grads[...] = jnp.zeros_like(tap_grads)
    fetch.wait()

    def correlate(b, _):
        first = half + b * UNIT
        for g in range(groups):
            cols = slice(g * LANES, (g + 1) * LANES)
            left = [grads[first + u, :, cols] for u in range(UNIT)]
            right = [scores[first + t, :, cols] for t in range(UNIT + count - 1)]
            for j in range(count):
                terms = [left[u] * right[u + j] for u in range(UNIT)]
                while len(terms) > 1:
                    terms = [terms[n] + terms[n + 1] for n in range(0, len(terms), 2)]
                tap_grads[j, :, cols] += terms[0]
        return 0

    lax.fori_loop(0, blk // UNIT, correlate, 0)
    tap_sums[:count, :] = jnp.sum(tap_grads[...], axis=1)
    tap_sums[count:, :] = jnp.zeros((tap_sums.shape[0] - count, query_count), F32)
    for copy in copies:
        copy.wait()


def column_block(frames, index, width):
    return frames[:, pl.ds(pl.multiple_of(index * width, LANES), width)]


def sum_kernel(arrived, taps_own, taps_far, taps_behind, taps_ahead, chunks, taps):
    tms, padded_rows, part_width = chunks.shape
    tall, query_count = taps.shape
    taps[...] = (taps_own[...] + taps_far[...]) + (taps_behind[...] + taps_ahead[...])
    chunk_rows = query_count // tms
    tap_blocks = tall // UNIT
    for z in range(tms):
        rows = slice(z * chunk_rows, (z + 1) * chunk_rows)
        total = arrived[0, rows, :]
        for r in range(1, arrived.shape[0]):
            total = total + arrived[r, rows, :]
        chunks[z, :chunk_rows, :] = total
        h, t = z // tap_blocks, z % tap_blocks
        if h * part_width < query_count:
            block = taps[t * UNIT : (t + 1) * UNIT, h * part_width : (h + 1) * part_width]
            chunks[z, chunk_rows:, :] = block
        else:
            chunks[z, chunk_rows:, :] = jnp.zeros((UNIT, part_width), F32)


def last_kernel(scale, whole, grad_queries, tap_sums):
    tms = whole.shape[0]
    query_count, part_width = grad_queries.shape
    count = tap_sums.shape[0]
    chunk_rows = query_count // tms
    blocks = padded_rows_of(count) // UNIT
    for z in range(tms):
        block = whole[z, :chunk_rows, :] * scale
        grad_queries[z * chunk_rows : (z + 1) * chunk_rows, :] = block.astype(jnp.bfloat16)
    for h in range(query_count // part_width):
        for t in range(blocks):
            used = min(UNIT, count - t * UNIT)
            tap_sums[t * UNIT : t * UNIT + used, h * part_width : (h + 1) * part_width] = whole[
                h * blocks + t, chunk_rows : chunk_rows + used, :
            ]


def padded_rows_of(count):
    return (count + UNIT - 1) // UNIT * UNIT


def per_device(frames, queries, kernel, labels, lengths):
    frame_rows = frames[0]
    rows, width = frame_rows.shape
    query_count = queries.shape[0]
    count = kernel.shape[0]
    half = count // 2
    rim = 2 * half
    blk = rows // SUB
    scale = 10.0 / math.sqrt(width)
    recs, tms, blocks = lax.axis_size("rec"), lax.axis_size("tm"), lax.axis_size("query")
    query_index = lax.axis_index("query")
    chips = blocks // 2
    chip, core = query_index // 2, query_index % 2
    keep_ids = [(chip + k) % chips * 2 + core for k in range(chips)]
    cross_ids = [(chip + k) % chips * 2 + 1 - core for k in range(chips)]
    scalars = jnp.stack(
        [lax.axis_index("tm") * rows, lengths[0], query_index * query_count] + keep_ids + cross_ids
    ).astype(jnp.int32)
    smem = pl.BlockSpec(memory_space=pltpu.SMEM)
    hbm = pl.BlockSpec(memory_space=pltpu.HBM)

    edge = jax.ShapeDtypeStruct((rim + UNIT, width), F32)
    last, first = pl.pallas_call(
        lambda *refs: edge_kernel(half, *refs),
        out_shape=[edge, edge],
        grid=(1,),
        in_specs=[
            pl.BlockSpec((rim, width), lambda i: (rows // rim - 1, 0)),
            pl.BlockSpec((rim, width), lambda i: (0, 0)),
            pl.BlockSpec(labels.shape, lambda i: (0, 0)),
        ],
        out_specs=[pl.BlockSpec(edge.shape, lambda i: (0, 0))] * 2,
        compiler_params=params(8),
        cost_estimate=cost(rim * width, 1 << 19),
    )(frame_rows, frame_rows, labels)
    up = [(i, i + 1) for i in range(tms - 1)]
    down = [(j, i) for i, j in up]
    before = lax.ppermute(last, "tm", up)
    after = lax.ppermute(first, "tm", down)
    steps = 4
    main = pl.pallas_call(
        lambda *refs: score_kernel(scale, steps, *refs),
        out_shape=jax.ShapeDtypeStruct((rows, query_count), F32),
        grid=(steps,),
        in_specs=[
            smem,
            pl.BlockSpec((rows, width // steps), lambda k: (0, k)),
            pl.BlockSpec((query_count, width // steps), lambda k: (0, k)),
        ],
        out_specs=pl.BlockSpec((rows, query_count), lambda k: (0, 0)),
        scratch_shapes=[VMEM((rows, rows), jnp.bfloat16)],
        compiler_params=params(16),
        cost_estimate=cost(2 * rows * width * (rows + query_count), 3 << 20),
    )(scalars, frame_rows, queries)
    main = main.reshape(blk, SUB, query_count)
    scores, powers, stats, tile = pl.pallas_call(
        lambda *refs: smooth_kernel(scale, half, *refs),
        out_shape=[
            jax.ShapeDtypeStruct((blk + 2 * rim, SUB, query_count), F32),
            jax.ShapeDtypeStruct((blk + rim, SUB, query_count), F32),
            jax.ShapeDtypeStruct((2, SUB, LANES), F32),
            jax.ShapeDtypeStruct((SUB, LANES), F32),
        ],
        in_specs=[smem] + whole_spec(6),
        out_specs=[hbm] + whole_spec(3),
        scratch_shapes=[
            VMEM((count, SUB, query_count), F32),
            VMEM((blk + 2 * rim, SUB, query_count), F32),
            pltpu.SemaphoreType.DMA(()),
        ],
        compiler_params=params(50),
        cost_estimate=cost(4 * rows * query_count * count, 6 << 20),
    )(scalars, main, before, after, labels, queries, kernel)
    others = lax.all_to_all(jnp.broadcast_to(stats[None], (blocks,) + stats.shape), "query", 0, 0)
    chunk_rows = query_count // tms
    part_width = width // recs
    out_width = width // blocks
    terms = jax.ShapeDtypeStruct((chips, rows, out_width), F32)
    parts, tap_sum, keep, cross = pl.pallas_call(
        lambda *refs: grad_kernel(half, *refs),
        out_shape=[
            jax.ShapeDtypeStruct((recs, query_count, part_width), F32),
            jax.ShapeDtypeStruct((padded_rows_of(count), query_count), F32),
            terms,
            terms,
        ],
        in_specs=[smem] + whole_spec(1) + [hbm] + whole_spec(6),
        out_specs=[hbm] + whole_spec(2) + [hbm],
        scratch_shapes=[
            VMEM((count, SUB, query_count), F32),
            VMEM((blk + rim, SUB, query_count), F32),
            VMEM((count, SUB, query_count), F32),
            VMEM((rows, query_count), jnp.bfloat16),
            VMEM((rows, width), F32),
            VMEM((recs, query_count, part_width), F32),
            VMEM(terms.shape, F32),
            VMEM(scores.shape, F32),
            pltpu.SemaphoreType.DMA((recs + 2,)),
        ],
        compiler_params=params(48),
        cost_estimate=cost(2 * rows * query_count * (width + 2 * count), 8 << 20),
    )(scalars, powers, scores, stats, others, tile, frame_rows, queries, kernel)
    parts = lax.all_to_all(parts, "rec", 0, 0)
    crossed = lax.ppermute(cross, "query", [(i, i ^ 1) for i in range(blocks)])
    far, behind, ahead = [
        lax.ppermute(tap_sum, "rec", [(i, (i + k) % recs) for i in range(recs)]) for k in (2, 1, 3)
    ]
    parts, keep, crossed = lax.optimization_barrier((parts, keep, crossed))
    chunks = pl.pallas_call(
        sum_kernel,
        out_shape=jax.ShapeDtypeStruct((tms, chunk_rows + UNIT, part_width), F32),
        in_specs=whole_spec(5),
        out_specs=pl.BlockSpec(memory_space=VMEM),
        scratch_shapes=[VMEM((padded_rows_of(count), query_count), F32)],
        compiler_params=params(8),
        cost_estimate=cost(4 * query_count * part_width, 4 << 20),
    )(parts, tap_sum, far, behind, ahead)
    chunk = jnp.sum(lax.all_to_all(chunks, "tm", 0, 0), axis=0)
    sends = [keep[k] + crossed[k] for k in range(chips)]
    frame_sum = sends[0]
    for k in range(1, chips):
        frame_sum = frame_sum + lax.ppermute(sends[k], "query", [(i, (i + 2 * k) % blocks) for i in range(blocks)])
    grad_frames = (frame_sum * scale).astype(jnp.bfloat16)[None]
    chunk, grad_frames = lax.optimization_barrier((chunk, grad_frames))
    whole = lax.all_gather(chunk, "tm")
    grad_queries, tap_sum = pl.pallas_call(
        lambda *refs: last_kernel(scale, *refs),
        out_shape=[
            jax.ShapeDtypeStruct((query_count, part_width), jnp.bfloat16),
            jax.ShapeDtypeStruct((count, query_count), F32),
        ],
        in_specs=whole_spec(1),
        out_specs=whole_spec(2),
        compiler_params=params(8),
        cost_estimate=cost(query_count * part_width, 1 << 20),
    )(whole)
    return (grad_frames, grad_queries, tap_sum)


def solution(mesh):
    in_specs = (P("rec", "tm", None), P("query", None), P(None, "query"), P("rec", "tm"), P("rec"))
    out_specs = (P("rec", "tm", "query"), P("query", "rec"), P(None, "query"))
    return jax.shard_map(
        per_device, mesh=mesh, in_specs=in_specs, out_specs=out_specs, check_vma=False
    )
```

```python
import math

import jax
import jax.numpy as jnp
from jax import lax
from jax.experimental import pallas as pl
from jax.experimental.pallas import tpu as pltpu
from jax.sharding import PartitionSpec as P

SUB = 8
LANES = 128
VMEM = pltpu.VMEM
F32 = jnp.float32
UNIT = 8


def whole_spec(count):
    return [pl.BlockSpec(memory_space=VMEM)] * count


def params(mib):
    return pltpu.CompilerParams(vmem_limit_bytes=mib << 20)


def cost(flops, bytes_accessed):
    return pl.CostEstimate(flops=flops, bytes_accessed=bytes_accessed, transcendentals=0)


def placement(rows, blk, flipped=False):
    m = lax.broadcasted_iota(jnp.int32, (rows, rows), 1 if flipped else 0)
    f = lax.broadcasted_iota(jnp.int32, (rows, rows), 0 if flipped else 1)
    return jnp.where(f == (m & (SUB - 1)) * blk + m // SUB, 1.0, 0.0).astype(jnp.bfloat16)


def dot_t(a, b):
    return lax.dot_general(a, b, (((1,), (1,)), ((), ())), preferred_element_type=F32)


def edge_kernel(half, last, first, labels, up, down):
    rim = 2 * half
    up[:rim, :] = last[...].astype(F32)
    down[:rim, :] = first[...].astype(F32)
    width = labels.shape[1]
    tail = labels[:, width - LANES :].astype(F32)
    up[rim:, :LANES] = jnp.broadcast_to(pltpu.roll(tail, half, 1), (UNIT, LANES))
    down[rim:, :LANES] = jnp.broadcast_to(labels[:, :LANES].astype(F32), (UNIT, LANES))


def score_kernel(scale, scalars, frames, queries, out):
    rows = frames.shape[0]
    blk = rows // SUB
    placed = jnp.dot(placement(rows, blk), frames[...], preferred_element_type=F32).astype(jnp.bfloat16)
    m = lax.broadcasted_iota(jnp.int32, (rows, 1), 0)
    frame = scalars[0] + (m & (SUB - 1)) * blk + m // SUB
    out[...] = jnp.where(frame < scalars[1], dot_t(placed, queries[...]) * scale, 0.0)


def label_tile(half, blk, labels, before, after):
    rim = 2 * half
    sub = lax.broadcasted_iota(jnp.int32, (SUB, LANES), 0)
    lane = lax.broadcasted_iota(jnp.int32, (SUB, LANES), 1)
    base = jnp.zeros((SUB, LANES), F32)
    for s in range(SUB):
        at = s * blk
        row = labels[:, at // LANES * LANES : at // LANES * LANES + LANES].astype(F32)
        row = jnp.broadcast_to(row, (SUB, LANES))
        if at % LANES:
            row = pltpu.roll(row, LANES - at % LANES, 1)
        base = jnp.where(sub == s, row, base)
    low = pltpu.roll(pltpu.roll(base, LANES - blk + half, 1), 1, 0)
    low = jnp.where(sub == 0, before[rim:, :LANES], low)
    high = pltpu.roll(pltpu.roll(base, half + blk, 1), SUB - 1, 0)
    high = jnp.where(sub == SUB - 1, pltpu.roll(after[rim:, :LANES], half + blk, 1), high)
    tile = jnp.where(lane < half, low, pltpu.roll(base, half, 1))
    return jnp.where(lane >= half + blk, high, tile)


def broadcast_taps(taps, wide, count):
    for j in range(count):
        wide[j] = jnp.broadcast_to(taps[j : j + 1, :], wide.shape[1:])


def tap_block(load, wide, g, count, flipped):
    sums = [None] * UNIT
    rows = [load(t) for t in range(UNIT + count - 1)]
    for j in range(count):
        tap = wide[count - 1 - j if flipped else j, :, g * LANES : (g + 1) * LANES]
        for u in range(UNIT):
            term = tap * rows[u + j]
            sums[u] = term if sums[u] is None else sums[u] + term
    return sums


def smooth_kernel(
    scale, half, scalars, main, before, after, labels, queries, taps, scores_out, powers, stats, tile, wide, scores, sem
):
    blk = main.shape[0]
    count = 2 * half + 1
    groups = queries.shape[0] // LANES
    rim = 2 * half
    broadcast_taps(taps, wide, count)
    tile[...] = label_tile(half, blk, labels, before, after)
    rim_frames = jnp.concatenate([before[:rim, :], after[:rim, :]], axis=0).astype(jnp.bfloat16)
    k = lax.broadcasted_iota(jnp.int32, (2 * rim, 1), 0)
    frame = scalars[0] + jnp.where(k < rim, k - rim, blk * SUB + k - rim)
    rim_scores = jnp.where(
        (frame >= 0) & (frame < scalars[1]), dot_t(rim_frames, queries[...]) * scale, 0.0
    )
    sub = lax.broadcasted_iota(jnp.int32, main.shape[1:], 0)
    scores[rim : rim + blk] = main[...]
    for t in range(rim):
        low = pltpu.roll(main[blk - rim + t], 1, 0)
        scores[t] = jnp.where(sub == 0, rim_scores[t : t + 1, :], low)
        high = pltpu.roll(main[t], SUB - 1, 0)
        scores[rim + blk + t] = jnp.where(sub == SUB - 1, rim_scores[rim + t : rim + t + 1, :], high)
    copy = pltpu.make_async_copy(scores, scores_out, sem)
    copy.start()
    lane = lax.broadcasted_iota(jnp.int32, (SUB, LANES), 1)

    def step(b, carry):
        tops, totals = carry
        first = b * UNIT
        tiles = []
        for g in range(groups):
            cols = slice(g * LANES, (g + 1) * LANES)
            tiles.append(tap_block(lambda t: scores[first + t, :, cols], wide, g, count, False))
        for u in range(UNIT):
            mine = [tiles[g][u] for g in range(groups)]
            peak = mine[0]
            for tile in mine[1:]:
                peak = jnp.maximum(peak, tile)
            top = jnp.max(peak, axis=1, keepdims=True)
            total = None
            for g in range(groups):
                e = jnp.exp(mine[g] - top)
                powers[first + u, :, g * LANES : (g + 1) * LANES] = e
                total = e if total is None else total + e
            total = jnp.sum(total, axis=1, keepdims=True)
            here = lane == first + u
            tops = jnp.where(here, top, tops)
            totals = jnp.where(here, total, totals)
        return tops, totals

    zero = jnp.zeros((SUB, LANES), F32)
    tops, totals = lax.fori_loop(0, (blk + rim) // UNIT, step, (zero, zero))
    stats[0] = tops
    stats[1] = totals
    copy.wait()


def grad_kernel(
    half, scalars, powers, scores_in, mine, others, labels, frames, queries, taps,
    chunks_out, tap_sums, keep_frames, cross_out, wide, grads, tap_grads, placed, frame_part, chunks, cross_frames, scores, sems,
):
    blk = powers.shape[0] - 2 * half
    rows = blk * SUB
    count = 2 * half + 1
    query_count = taps.shape[1]
    groups = query_count // LANES
    fetch = pltpu.make_async_copy(scores_in, scores, sems.at[sems.shape[0] - 1])
    fetch.start()
    broadcast_taps(taps, wide, count)
    tops = others[:, 0]
    top = jnp.max(tops, axis=0)
    total = jnp.sum(others[:, 1] * jnp.exp(tops - top[None]), axis=0)
    lane = lax.broadcasted_iota(jnp.int32, (SUB, LANES), 1)
    frame = scalars[0] + lax.broadcasted_iota(jnp.int32, (SUB, LANES), 0) * blk + lane - half
    valid = (frame >= 0) & (frame < scalars[1]) & (lane < blk + 2 * half)
    weight = jnp.where(valid, jnp.exp(mine[0] - top) / total, 0.0)
    label = jnp.where(valid, labels[...] - scalars[2].astype(F32), -1.0)
    keep = jnp.where(valid, 1.0, 0.0)
    ids = lax.broadcasted_iota(jnp.int32, (SUB, query_count), 1).astype(F32)

    def place(b, _):
        first = b * UNIT
        turn = lax.rem(LANES - first, LANES)
        w = pltpu.roll(weight, turn, 1)
        l = pltpu.roll(label, turn, 1)
        for u in range(UNIT):
            positive = jnp.where(ids == l[:, u : u + 1], 1.0, 0.0)
            grads[first + u] = powers[first + u] * w[:, u : u + 1] - positive
        return 0

    lax.fori_loop(0, (blk + 2 * half) // UNIT, place, 0)

    def spread(b, _):
        first = b * UNIT
        turn = lax.rem(2 * LANES - half - first, LANES)
        kept = pltpu.roll(keep, turn, 1)
        for g in range(groups):
            cols = slice(g * LANES, (g + 1) * LANES)
            sums = tap_block(lambda t: grads[first + t, :, cols], wide, g, count, True)
            sums = [sums[u] * kept[:, u : u + 1] for u in range(UNIT)]
            block = jnp.concatenate(sums, axis=0).astype(jnp.bfloat16)
            placed[pl.ds(pl.multiple_of(first * SUB, UNIT * SUB), UNIT * SUB), cols] = block
        return 0

    lax.fori_loop(0, blk // UNIT, spread, 0)
    natural = jnp.dot(placement(rows, blk, True), placed[...], preferred_element_type=F32)
    turned = natural.T.astype(jnp.bfloat16)
    natural = natural.astype(jnp.bfloat16)
    recs, part_rows, part_width = chunks.shape
    copies = []
    for r in range(recs):
        chunks[r] = jnp.dot(turned, frames[:, r * part_width : (r + 1) * part_width], preferred_element_type=F32)
        copies.append(pltpu.make_async_copy(chunks.at[r], chunks_out.at[r], sems.at[r]))
        copies[r].start()
    frame_part[...] = jnp.dot(natural, queries[...], preferred_element_type=F32)
    chips, _, out_width = keep_frames.shape
    for k in range(chips):
        keep_frames[k] = column_block(frame_part, scalars[3 + k], out_width)
        cross_frames[k] = column_block(frame_part, scalars[3 + chips + k], out_width)
    copies.append(pltpu.make_async_copy(cross_frames, cross_out, sems.at[recs]))
    copies[recs].start()
    tap_grads[...] = jnp.zeros_like(tap_grads)
    fetch.wait()

    def correlate(b, _):
        first = half + b * UNIT
        for g in range(groups):
            cols = slice(g * LANES, (g + 1) * LANES)
            left = [grads[first + u, :, cols] for u in range(UNIT)]
            right = [scores[first + t, :, cols] for t in range(UNIT + count - 1)]
            for j in range(count):
                terms = [left[u] * right[u + j] for u in range(UNIT)]
                while len(terms) > 1:
                    terms = [terms[n] + terms[n + 1] for n in range(0, len(terms), 2)]
                tap_grads[j, :, cols] += terms[0]
        return 0

    lax.fori_loop(0, blk // UNIT, correlate, 0)
    tap_sums[:count, :] = jnp.sum(tap_grads[...], axis=1)
    tap_sums[count:, :] = jnp.zeros((tap_sums.shape[0] - count, query_count), F32)
    for copy in copies:
        copy.wait()


def column_block(frames, index, width):
    return frames[:, pl.ds(pl.multiple_of(index * width, LANES), width)]


def sum_kernel(arrived, taps_own, taps_far, taps_behind, taps_ahead, chunks, taps):
    tms, padded_rows, part_width = chunks.shape
    tall, query_count = taps.shape
    taps[...] = (taps_own[...] + taps_far[...]) + (taps_behind[...] + taps_ahead[...])
    chunk_rows = query_count // tms
    tap_blocks = tall // UNIT
    for z in range(tms):
        rows = slice(z * chunk_rows, (z + 1) * chunk_rows)
        total = arrived[0, rows, :]
        for r in range(1, arrived.shape[0]):
            total = total + arrived[r, rows, :]
        chunks[z, :chunk_rows, :] = total
        h, t = z // tap_blocks, z % tap_blocks
        if h * part_width < query_count:
            block = taps[t * UNIT : (t + 1) * UNIT, h * part_width : (h + 1) * part_width]
            chunks[z, chunk_rows:, :] = block
        else:
            chunks[z, chunk_rows:, :] = jnp.zeros((UNIT, part_width), F32)


def last_kernel(scale, whole, grad_queries, tap_sums):
    tms = whole.shape[0]
    query_count, part_width = grad_queries.shape
    count = tap_sums.shape[0]
    chunk_rows = query_count // tms
    blocks = padded_rows_of(count) // UNIT
    for z in range(tms):
        block = whole[z, :chunk_rows, :] * scale
        grad_queries[z * chunk_rows : (z + 1) * chunk_rows, :] = block.astype(jnp.bfloat16)
    for h in range(query_count // part_width):
        for t in range(blocks):
            used = min(UNIT, count - t * UNIT)
            tap_sums[t * UNIT : t * UNIT + used, h * part_width : (h + 1) * part_width] = whole[
                h * blocks + t, chunk_rows : chunk_rows + used, :
            ]


def padded_rows_of(count):
    return (count + UNIT - 1) // UNIT * UNIT


def per_device(frames, queries, kernel, labels, lengths):
    frame_rows = frames[0]
    rows, width = frame_rows.shape
    query_count = queries.shape[0]
    count = kernel.shape[0]
    half = count // 2
    rim = 2 * half
    blk = rows // SUB
    scale = 10.0 / math.sqrt(width)
    recs, tms, blocks = lax.axis_size("rec"), lax.axis_size("tm"), lax.axis_size("query")
    query_index = lax.axis_index("query")
    chips = blocks // 2
    chip, core = query_index // 2, query_index % 2
    keep_ids = [(chip + k) % chips * 2 + core for k in range(chips)]
    cross_ids = [(chip + k) % chips * 2 + 1 - core for k in range(chips)]
    scalars = jnp.stack(
        [lax.axis_index("tm") * rows, lengths[0], query_index * query_count] + keep_ids + cross_ids
    ).astype(jnp.int32)
    smem = pl.BlockSpec(memory_space=pltpu.SMEM)
    hbm = pl.BlockSpec(memory_space=pltpu.HBM)

    edge = jax.ShapeDtypeStruct((rim + UNIT, width), F32)
    last, first = pl.pallas_call(
        lambda *refs: edge_kernel(half, *refs),
        out_shape=[edge, edge],
        grid=(1,),
        in_specs=[
            pl.BlockSpec((rim, width), lambda i: (rows // rim - 1, 0)),
            pl.BlockSpec((rim, width), lambda i: (0, 0)),
            pl.BlockSpec(labels.shape, lambda i: (0, 0)),
        ],
        out_specs=[pl.BlockSpec(edge.shape, lambda i: (0, 0))] * 2,
        compiler_params=params(8),
        cost_estimate=cost(rim * width, 1 << 19),
    )(frame_rows, frame_rows, labels)
    up = [(i, i + 1) for i in range(tms - 1)]
    down = [(j, i) for i, j in up]
    before = lax.ppermute(last, "tm", up)
    after = lax.ppermute(first, "tm", down)
    main = pl.pallas_call(
        lambda *refs: score_kernel(scale, *refs),
        out_shape=jax.ShapeDtypeStruct((rows, query_count), F32),
        in_specs=[smem] + whole_spec(2),
        out_specs=pl.BlockSpec(memory_space=VMEM),
        compiler_params=params(12),
        cost_estimate=cost(2 * rows * width * (rows + query_count), 3 << 20),
    )(scalars, frame_rows, queries)
    main = main.reshape(blk, SUB, query_count)
    scores, powers, stats, tile = pl.pallas_call(
        lambda *refs: smooth_kernel(scale, half, *refs),
        out_shape=[
            jax.ShapeDtypeStruct((blk + 2 * rim, SUB, query_count), F32),
            jax.ShapeDtypeStruct((blk + rim, SUB, query_count), F32),
            jax.ShapeDtypeStruct((2, SUB, LANES), F32),
            jax.ShapeDtypeStruct((SUB, LANES), F32),
        ],
        in_specs=[smem] + whole_spec(6),
        out_specs=[hbm] + whole_spec(3),
        scratch_shapes=[
            VMEM((count, SUB, query_count), F32),
            VMEM((blk + 2 * rim, SUB, query_count), F32),
            pltpu.SemaphoreType.DMA(()),
        ],
        compiler_params=params(50),
        cost_estimate=cost(4 * rows * query_count * count, 6 << 20),
    )(scalars, main, before, after, labels, queries, kernel)
    others = lax.all_to_all(jnp.broadcast_to(stats[None], (blocks,) + stats.shape), "query", 0, 0)
    chunk_rows = query_count // tms
    part_width = width // recs
    out_width = width // blocks
    terms = jax.ShapeDtypeStruct((chips, rows, out_width), F32)
    parts, tap_sum, keep, cross = pl.pallas_call(
        lambda *refs: grad_kernel(half, *refs),
        out_shape=[
            jax.ShapeDtypeStruct((recs, query_count, part_width), F32),
            jax.ShapeDtypeStruct((padded_rows_of(count), query_count), F32),
            terms,
            terms,
        ],
        in_specs=[smem] + whole_spec(1) + [hbm] + whole_spec(6),
        out_specs=[hbm] + whole_spec(2) + [hbm],
        scratch_shapes=[
            VMEM((count, SUB, query_count), F32),
            VMEM((blk + rim, SUB, query_count), F32),
            VMEM((count, SUB, query_count), F32),
            VMEM((rows, query_count), jnp.bfloat16),
            VMEM((rows, width), F32),
            VMEM((recs, query_count, part_width), F32),
            VMEM(terms.shape, F32),
            VMEM(scores.shape, F32),
            pltpu.SemaphoreType.DMA((recs + 2,)),
        ],
        compiler_params=params(48),
        cost_estimate=cost(2 * rows * query_count * (width + 2 * count), 8 << 20),
    )(scalars, powers, scores, stats, others, tile, frame_rows, queries, kernel)
    parts = lax.all_to_all(parts, "rec", 0, 0)
    crossed = lax.ppermute(cross, "query", [(i, i ^ 1) for i in range(blocks)])
    far, behind, ahead = [
        lax.ppermute(tap_sum, "rec", [(i, (i + k) % recs) for i in range(recs)]) for k in (2, 1, 3)
    ]
    parts, keep, crossed = lax.optimization_barrier((parts, keep, crossed))
    chunks = pl.pallas_call(
        sum_kernel,
        out_shape=jax.ShapeDtypeStruct((tms, chunk_rows + UNIT, part_width), F32),
        in_specs=whole_spec(5),
        out_specs=pl.BlockSpec(memory_space=VMEM),
        scratch_shapes=[VMEM((padded_rows_of(count), query_count), F32)],
        compiler_params=params(8),
        cost_estimate=cost(4 * query_count * part_width, 4 << 20),
    )(parts, tap_sum, far, behind, ahead)
    chunk = jnp.sum(lax.all_to_all(chunks, "tm", 0, 0), axis=0)
    sends = [keep[k] + crossed[k] for k in range(chips)]
    frame_sum = sends[0]
    for k in range(1, chips):
        frame_sum = frame_sum + lax.ppermute(sends[k], "query", [(i, (i + 2 * k) % blocks) for i in range(blocks)])
    grad_frames = (frame_sum * scale).astype(jnp.bfloat16)[None]
    chunk, grad_frames = lax.optimization_barrier((chunk, grad_frames))
    whole = lax.all_gather(chunk, "tm")
    grad_queries, tap_sum = pl.pallas_call(
        lambda *refs: last_kernel(scale, *refs),
        out_shape=[
            jax.ShapeDtypeStruct((query_count, part_width), jnp.bfloat16),
            jax.ShapeDtypeStruct((count, query_count), F32),
        ],
        in_specs=whole_spec(1),
        out_specs=whole_spec(2),
        compiler_params=params(8),
        cost_estimate=cost(query_count * part_width, 1 << 20),
    )(whole)
    return (grad_frames, grad_queries, tap_sum)


def solution(mesh):
    in_specs = (P("rec", "tm", None), P("query", None), P(None, "query"), P("rec", "tm"), P("rec"))
    out_specs = (P("rec", "tm", "query"), P("query", "rec"), P(None, "query"))
    return jax.shard_map(
        per_device, mesh=mesh, in_specs=in_specs, out_specs=out_specs, check_vma=False
    )
```
